32 devices in a mesh: group: 2 (over y), det: 4 (over z), tm: 2 (over x), pol: 2 (over core).
Axes of the slice: x: 2, y: 2, z: 4, core: 2. Of those that a mesh axis runs over, the one named last changes fastest.
Arguments:
- timestream: bfloat16 [128, 16384], P(('group', 'det', 'pol'), 'tm'), parts along dimension 0, may hold values from -6 to 6
- hwp_index: int32 [32768], P(('group', 'tm')), parts along dimension 0, may hold values from 0 to 8191
- flags: int32 [128, 16384], P(('group', 'det', 'pol'), 'tm'), parts along dimension 0, may hold values 0 or 1
- pixel_index: int32 [128, 16384], P(('group', 'det', 'pol'), 'tm'), parts along dimension 0, may hold values from 0 to 16383, as said below
- tile_index: int32 [128, 32], P(('group', 'det', 'pol'), 'tm'), parts along dimension 0, may hold values from 0 to 15
- wafer: int32 [128], P(('group', 'det', 'pol')), parts along dimension 0, may hold values from 0 to 6
- taps: float32 [7, 33], replicated, may hold values from -1 to 1
- detector_angle: float32 [128], P(('group', 'det', 'pol')), parts along dimension 0, may hold values from -3.140625 to 3.140625
Outputs:
- e_modes: float32 [2, 1024, 512], P(None, ('group', 'det', 'tm', 'pol')), parts along dimension 1
- b_modes: float32 [2, 1024, 512], P(None, ('group', 'det', 'tm', 'pol')), parts along dimension 1
The draws below stay inside these ranges and needn't reach their ends.
There are 2 independent parts, one for each index of `group`. The reference program is written for one: setup_inputs(seed, part) draws one part's arguments, and reference() takes and returns one part's arrays. A program takes and returns all parts, laid end to end along the dimension named above; an argument that names none is the same for every part. Nothing has to cross between parts.
Inputs may be any that keep to these rules, and one draw needn't show every extreme that they name: `pixel_index`: position inside a tile, row-major; in each pointing block of 512 samples of one detector, exactly 128 samples lie in each band of 32 consecutive tile rows.
All inputs are finite; a program needn't handle non-finite values. No bound on the sum of `flags` on one device may be relied on, other than what follows from the above.
Results may differ from the reference program's by a relative error of at most 0.0029.
Values may be sent and summed in bfloat16 or wider, within the bound.
A program may use at most 64 MiB of HBM per device.

```python
import math
import jax
import jax.numpy as jnp

DET_DEV = 8
TS_DEV = 8192
BLK = 512
TILE = 128
MAPY = 2048
KY = 512
HALF = 16
NWAF = 7
NANG = 8192
TAPS = 33
DETS = 64
SAMPLES = 16384
NBLK = 32
MAPX = 512
N_DET = 4
N_POL = 2


def block_order(block_key):
    return jax.random.permutation(block_key, BLK)


def draw_pixel_index(key, part):
    key = jax.random.fold_in(key, 11)
    band_rows = TILE // N_DET
    block_keys = jax.random.split(jax.random.fold_in(key, 1), DETS * NBLK)
    orders = jax.vmap(block_order)(block_keys)
    band = (orders % N_DET).reshape(DETS, SAMPLES)
    inner = jax.random.randint(jax.random.fold_in(key, 2), (DETS, SAMPLES), 0, band_rows)
    column = jax.random.randint(jax.random.fold_in(key, 3), (DETS, SAMPLES), 0, TILE)
    return ((band * band_rows + inner) * TILE + column).astype(jnp.int32)


def place_ends(values, rng, least, top_value):
    longest = values.shape.index(max(values.shape))
    spots = []
    for shift in (0, 1):
        where = [jax.random.randint(jax.random.fold_in(rng, axis), (), 0, length) for axis, length in enumerate(values.shape)]
        where[longest] = (where[longest] + shift) % values.shape[longest]
        spots.append(tuple(where))
    return values.at[spots[0]].set(least).at[spots[1]].set(top_value)


def level_of(rng, extent, pieces, smallest, top_value):
    factor_of, own = 1.0, jax.random.fold_in(rng, 6)
    for axis_at, shards_of in pieces:
        heights = jnp.exp(jax.random.uniform(jax.random.fold_in(own, axis_at), (shards_of,), jnp.float32, smallest / len(pieces), top_value / len(pieces)))
        factor_of = factor_of * jnp.repeat(heights, extent[axis_at] // shards_of).reshape([-1 if axis == axis_at else 1 for axis in range(len(extent))])
    return factor_of


def centred(rng, extent, spread, bound, cuts=(), held_as=jnp.bfloat16):
    drawn = spread * jax.random.normal(rng, extent, jnp.float32)
    if cuts:
        drawn = drawn * level_of(rng, extent, cuts, -0.22, 0.18)
    return jnp.clip(drawn, -bound, bound).astype(held_as)


def setup_inputs(seed: int = 0, part: int = 0) -> dict:
    arg_keys = jax.random.split(jax.random.key(seed), 9)
    part_keys = jax.random.split(jax.random.fold_in(arg_keys[8], part), 9)
    timestream = centred(part_keys[0], (DETS, SAMPLES), 1.0, 6.0, ((0, 8), (1, 2)))
    hwp_index = place_ends(jax.random.randint(part_keys[1], (SAMPLES,), 0, NANG), jax.random.fold_in(part_keys[1], 1), 0, NANG - 1).astype(jnp.int32)
    flags = place_ends((jax.random.randint(part_keys[2], (DETS, SAMPLES), 0, 8) < 7).astype(jnp.int32), jax.random.fold_in(part_keys[2], 1), 0, 1)
    pixel_index = draw_pixel_index(jax.random.fold_in(jax.random.fold_in(arg_keys[8], part), 71), part)
    tile_index = place_ends(jax.random.randint(part_keys[4], (DETS, NBLK), 0, MAPY // TILE), jax.random.fold_in(part_keys[4], 1), 0, (MAPY // TILE) - 1).astype(jnp.int32)
    wafer = place_ends(jax.random.randint(part_keys[5], (DETS,), 0, NWAF), jax.random.fold_in(part_keys[5], 1), 0, NWAF - 1).astype(jnp.int32)
    taps = centred(arg_keys[6], (NWAF, TAPS), TAPS ** -0.5, 1.0, (), jnp.float32)
    detector_angle = jnp.clip(jax.random.uniform(part_keys[7], (DETS,), jnp.float32, -3.140625, 3.140625), -3.140625, 3.140625)
    return {"timestream": timestream, "hwp_index": hwp_index, "flags": flags, "pixel_index": pixel_index, "tile_index": tile_index, "wafer": wafer, "taps": taps, "detector_angle": detector_angle}


def reference(timestream, hwp_index, flags, pixel_index, tile_index, wafer, taps, detector_angle):
    det_count, sample_count = timestream.shape
    det_taps = taps[wafer]
    padded = jnp.pad(timestream.astype(jnp.float32), ((0, 0), (HALF, HALF)))
    filtered = jnp.zeros((det_count, sample_count), jnp.float32)
    for offset in range(2 * HALF + 1):
        filtered = filtered + det_taps[:, offset:offset + 1] * padded[:, offset:offset + sample_count]
    hwp_turns = (4 * hwp_index % NANG).astype(jnp.float32) * (2.0 * math.pi / NANG)
    demod_phase = hwp_turns[None, :] - 2.0 * detector_angle[:, None]
    flagged = filtered * flags.astype(jnp.float32)
    q_values = (flagged * jnp.cos(demod_phase)).astype(jnp.bfloat16)
    u_values = (flagged * jnp.sin(demod_phase)).astype(jnp.bfloat16)
    det_pos = jnp.arange(det_count, dtype=jnp.int32)[:, None]
    time_pos = jnp.arange(sample_count, dtype=jnp.int32)[None, :]
    strip = time_pos // TS_DEV * N_POL + det_pos // DET_DEV % N_POL
    row_pos = strip * TILE + pixel_index // TILE
    block_tile = jnp.repeat(tile_index, BLK, axis=1)
    col_pos = block_tile * TILE + pixel_index % TILE
    maps = jnp.zeros((2, MAPX, MAPY), jnp.float32)
    maps = maps.at[0, row_pos, col_pos].add(q_values.astype(jnp.float32))
    maps = maps.at[1, row_pos, col_pos].add(u_values.astype(jnp.float32))
    spectrum = jnp.fft.fft2(maps, axes=(1, 2))[:, :, :KY] / math.sqrt(MAPX * MAPY)
    q_hat = jnp.transpose(spectrum[0])
    u_hat = jnp.transpose(spectrum[1])
    kx_pos = jnp.arange(MAPX, dtype=jnp.int32)
    freq_x = jnp.where(kx_pos < MAPX // 2, kx_pos, kx_pos - MAPX).astype(jnp.float32)[None, :]
    freq_y = jnp.arange(KY, dtype=jnp.int32).astype(jnp.float32)[:, None]
    radius = jnp.maximum(freq_x * freq_x + freq_y * freq_y, 1.0)
    cosine = (freq_x * freq_x - freq_y * freq_y) / radius
    sine = 2.0 * freq_x * freq_y / radius
    e_hat = cosine * q_hat + sine * u_hat
    b_hat = cosine * u_hat - sine * q_hat
    e_modes = jnp.stack([jnp.real(e_hat), jnp.imag(e_hat)]).astype(jnp.float32)
    b_modes = jnp.stack([jnp.real(b_hat), jnp.imag(b_hat)]).astype(jnp.float32)
    return (e_modes, b_modes)
```

```python
import math

import jax
import jax.numpy as jnp
import ml_dtypes
import numpy as np
from jax import lax
from jax.experimental import pallas as pl
from jax.experimental.pallas import tpu as pltpu
from jax.sharding import PartitionSpec as P

TILE = 128
MAPY = 2048
KY = 512
NANG = 8192
LANES = 128
CHUNK = 1024
HIGH = lax.Precision.HIGHEST
MESH = pl.DeviceIdType.MESH
NT = (((1,), (1,)), ((), ()))


def split_np(table):
    table = table.astype(np.float32)
    high = table.astype(ml_dtypes.bfloat16)
    low = (table - high.astype(np.float32)).astype(ml_dtypes.bfloat16)
    return high, low


def split(value):
    high = value.astype(jnp.bfloat16)
    return high, (value - high.astype(jnp.float32)).astype(jnp.bfloat16)


def row_tables(owners):
    kept = KY // owners
    ky = np.arange(KY).reshape(owners, 1, kept // 2, 2)
    ky = np.moveaxis(ky, 3, 0)
    y = np.arange(MAPY // 2)
    angle = (ky[..., None] * y % MAPY) * (2.0 * np.pi / MAPY)
    table = np.concatenate([np.cos(angle), -np.sin(angle)], axis=2)
    return split_np(table.reshape(2, KY, MAPY // 2))


def column_tables(length):
    pos = np.arange(length)
    angle = (pos[:, None] * pos[None, :] % length) * (2.0 * np.pi / length)
    table = np.concatenate([np.cos(angle), np.sin(angle)], axis=1)
    return split_np(table / math.sqrt(length * MAPY))


def halos(block, width):
    count = lax.axis_size("tm")
    forward = [(i, i + 1) for i in range(count - 1)]
    backward = [(target, source) for source, target in forward]
    low = lax.ppermute(block[:, block.shape[1] - width :], "tm", forward)
    high = lax.ppermute(block[:, :width], "tm", backward)
    return low, high


def bin_kernel(
    tile_ref, ts_ref, low_ref, high_ref, hwp_ref, flags_ref, pix_ref, wafer_ref, taps_ref,
    angle_ref, thigh_ref, tlow_ref, out_ref,
    xs, cos_h, sin_h, q_s, u_s, map_s,
):
    det_rows, time_len = ts_ref.shape
    tap_count = taps_ref.shape[1]
    width = (tap_count - 1) // 2
    block_count = tile_ref.shape[1]
    block_len = time_len // block_count

    xs[:, 0:LANES] = jnp.zeros((det_rows, LANES), jnp.float32)
    xs[:, LANES + time_len :] = jnp.zeros((det_rows, LANES), jnp.float32)
    xs[:, LANES : LANES + time_len] = ts_ref[...].astype(jnp.float32)
    xs[:, LANES - width : LANES] = low_ref[...].astype(jnp.float32)
    xs[:, LANES + time_len : LANES + time_len + width] = high_ref[...].astype(jnp.float32)
    wafer = wafer_ref[...]
    det_taps = jnp.zeros((det_rows, tap_count), jnp.float32)
    for w in range(taps_ref.shape[0]):
        det_taps = det_taps + jnp.where(wafer == w, taps_ref[w : w + 1, :], 0.0)
    hwp = (4 * hwp_ref[...] % NANG).astype(jnp.float32) * (2.0 * math.pi / NANG)
    cos_h[...] = jnp.cos(hwp)
    sin_h[...] = jnp.sin(hwp)
    twice = 2.0 * angle_ref[...]
    cos_a = jnp.cos(twice)
    sin_a = jnp.sin(twice)
    chunk = min(CHUNK, time_len)
    span = chunk + 2 * LANES
    per = chunk // LANES

    @pl.loop(0, time_len // chunk)
    def _(step):
        start = pl.multiple_of(step * chunk, chunk)
        base = xs[:, pl.ds(start, span)]
        total = jnp.zeros((det_rows, chunk), jnp.float32)
        for j in range(tap_count):
            moved = pltpu.roll(base, span - (LANES - width + j), 1)
            total = total + det_taps[:, j : j + 1] * moved[:, :chunk]
        flagged = total * flags_ref[:, pl.ds(start, chunk)].astype(jnp.float32)
        rows = pl.ds(pl.multiple_of(step * per, per), per)
        ch = cos_h[rows, :]
        sh = sin_h[rows, :]
        for k in range(per):
            lanes = pl.ds(pl.multiple_of(start + k * LANES, LANES), LANES)
            part = flagged[:, k * LANES : (k + 1) * LANES]
            c = ch[k : k + 1, :]
            s = sh[k : k + 1, :]
            q_s[:, lanes] = part * (c * cos_a + s * sin_a)
            u_s[:, lanes] = part * (s * cos_a - c * sin_a)

    map_s[...] = jnp.zeros(map_s.shape, jnp.float32)
    sub = 16
    side = lax.broadcasted_iota(jnp.int32, (sub, block_len), 0).astype(jnp.float32)
    zero = jnp.zeros((sub, block_len), jnp.bfloat16)
    one = jnp.ones((sub, block_len), jnp.bfloat16)
    ids = [(side + float(g * sub)).astype(jnp.bfloat16) for g in range(TILE // sub)]

    def spread(row):
        return jnp.broadcast_to(row, (sub, block_len)).astype(jnp.bfloat16)

    @pl.loop(0, block_count)
    def _(b):
        lanes = pl.ds(pl.multiple_of(b * block_len, block_len), block_len)
        for d in range(det_rows):
            pix = pix_ref[d : d + 1, lanes]
            row_id = spread((pix // TILE).astype(jnp.float32))
            col_id = spread((pix % TILE).astype(jnp.float32))
            qv = spread(q_s[d : d + 1, lanes])
            uv = spread(u_s[d : d + 1, lanes])
            hits = [row_id == i for i in ids]
            weighted = jnp.concatenate(
                [jnp.where(h, qv, zero) for h in hits] + [jnp.where(h, uv, zero) for h in hits],
                axis=0,
            )
            col_hot = jnp.concatenate([jnp.where(col_id == i, one, zero) for i in ids], axis=0)
            sums = lax.dot_general(weighted, col_hot, NT, preferred_element_type=jnp.float32)
            tile = tile_ref[d, b]
            map_s[tile] = map_s[tile] + sums

    tiles = MAPY // TILE
    first = jnp.concatenate([map_s[t] for t in range(tiles // 2)], axis=1)
    second = jnp.concatenate([map_s[t] for t in range(tiles // 2, tiles)], axis=1)
    for parity in range(2):
        folded = first + second if parity == 0 else first - second
        f_high, f_low = split(folded)
        t_high = thigh_ref[parity]
        acc = lax.dot_general(t_high, f_high, NT, preferred_element_type=jnp.float32)
        acc = acc + lax.dot_general(t_high, f_low, NT, preferred_element_type=jnp.float32)
        acc = acc + lax.dot_general(
            tlow_ref[parity], f_high, NT, preferred_element_type=jnp.float32
        )
        out_ref[2 * parity] = acc[:, :TILE].astype(jnp.bfloat16)
        out_ref[2 * parity + 1] = acc[:, TILE:].astype(jnp.bfloat16)


def local_spectrum(timestream, hwp_index, flags, pixel_index, tile_index, wafer, taps, angle, owners):
    det_rows, time_len = timestream.shape
    width = (taps.shape[1] - 1) // 2
    low, high = halos(timestream, width)
    t_high, t_low = row_tables(owners)
    vmem = pl.BlockSpec(memory_space=pltpu.VMEM)
    return pl.pallas_call(
        bin_kernel,
        out_shape=jax.ShapeDtypeStruct((4, KY, TILE), jnp.bfloat16),
        in_specs=[pl.BlockSpec(memory_space=pltpu.SMEM)] + [vmem] * 11,
        out_specs=vmem,
        scratch_shapes=[
            pltpu.VMEM((det_rows, time_len + 2 * LANES), jnp.float32),
            pltpu.VMEM((time_len // LANES, LANES), jnp.float32),
            pltpu.VMEM((time_len // LANES, LANES), jnp.float32),
            pltpu.VMEM((det_rows, time_len), jnp.float32),
            pltpu.VMEM((det_rows, time_len), jnp.float32),
            pltpu.VMEM((MAPY // TILE, 2 * TILE, TILE), jnp.float32),
        ],
        compiler_params=pltpu.CompilerParams(vmem_limit_bytes=40 * 2**20),
        name="bin_and_rows",
    )(
        tile_index, timestream, low, high, hwp_index.reshape(time_len // LANES, LANES), flags,
        pixel_index, wafer[:, None], taps, angle[:, None], jnp.asarray(t_high), jnp.asarray(t_low),
    )


def rotation(kx, length, ky):
    fx = jnp.where(kx < length // 2, kx, kx - length).astype(jnp.float32)
    fy = ky.astype(jnp.float32)
    radius = jnp.maximum(fx * fx + fy * fy, 1.0)
    return (fx * fx - fy * fy) / radius, 2.0 * fx * fy / radius


def exchange_kernel(sizes, spec_ref, whigh_ref, wlow_ref, e_ref, b_ref, recv, ordered, send_sem, recv_sem):
    n_det, n_tm, n_pol = sizes
    owners = n_det * n_tm * n_pol
    strips = n_tm * n_pol
    kept = KY // owners
    half = kept // 2
    length = strips * TILE
    me = (lax.axis_index("det") * n_tm + lax.axis_index("tm")) * n_pol + lax.axis_index("pol")

    def place(index):
        return {
            "det": index // strips,
            "tm": lax.rem(index // n_pol, n_tm),
            "pol": lax.rem(index, n_pol),
        }

    barrier = pltpu.get_barrier_semaphore()
    for step in range(1, owners):
        peer = lax.rem(me + step, owners)
        pl.semaphore_signal(barrier, inc=1, device_id=place(peer), device_id_type=MESH)
    pl.semaphore_wait(barrier, owners - 1)

    copies = []
    for step in range(1, owners):
        peer = lax.rem(me + step, owners)
        copy = pltpu.make_async_remote_copy(
            src_ref=spec_ref.at[:, pl.ds(pl.multiple_of(peer * kept, kept), kept), :],
            dst_ref=recv.at[me],
            send_sem=send_sem.at[step],
            recv_sem=recv_sem.at[step],
            device_id=place(peer),
            device_id_type=MESH,
        )
        copy.start()
        copies.append(copy)
    recv[me] = spec_ref[:, pl.ds(pl.multiple_of(me * kept, kept), kept), :]
    kx = lax.broadcasted_iota(jnp.int32, (kept, length), 1)
    ky = me * kept + lax.broadcasted_iota(jnp.int32, (kept, length), 0)
    cosine, sine = rotation(kx, length, ky)
    for copy in copies:
        copy.wait()

    columns = []
    for strip in range(strips):
        total = recv[strip].astype(jnp.float32)
        for det in range(1, n_det):
            total = total + recv[det * strips + strip].astype(jnp.float32)
        for parity in range(2):
            for c in range(2):
                for part in range(2):
                    ordered[strip, c, part, pl.ds(parity, half, stride=2), :] = total[
                        2 * parity + c, part * half : (part + 1) * half
                    ]
        columns.append(ordered[strip].reshape(4 * kept, TILE))
    x_high, x_low = split(jnp.concatenate(columns, axis=1))
    w_high = whigh_ref[...]
    acc = jnp.dot(x_high, w_high, preferred_element_type=jnp.float32)
    acc = acc + jnp.dot(x_low, w_high, preferred_element_type=jnp.float32)
    acc = acc + jnp.dot(x_high, wlow_ref[...], preferred_element_type=jnp.float32)
    real, imag = [], []
    for c in range(2):
        re_rows = slice(2 * c * kept, (2 * c + 1) * kept)
        im_rows = slice((2 * c + 1) * kept, (2 * c + 2) * kept)
        real.append(acc[re_rows, :length] + acc[im_rows, length:])
        imag.append(acc[im_rows, :length] - acc[re_rows, length:])
    e_ref[0] = cosine * real[0] + sine * real[1]
    e_ref[1] = cosine * imag[0] + sine * imag[1]
    b_ref[0] = cosine * real[1] - sine * real[0]
    b_ref[1] = cosine * imag[1] - sine * imag[0]


def exchange(spec, sizes):
    owners = math.prod(sizes)
    kept = KY // owners
    length = sizes[1] * sizes[2] * TILE
    w_high, w_low = column_tables(length)
    vmem = pl.BlockSpec(memory_space=pltpu.VMEM)
    shape = jax.ShapeDtypeStruct((2, kept, length), jnp.float32)

    def kernel(*refs):
        exchange_kernel(sizes, *refs)

    return pl.pallas_call(
        kernel,
        out_shape=(shape, shape),
        in_specs=[vmem] * 3,
        out_specs=(vmem, vmem),
        scratch_shapes=[
            pltpu.VMEM((owners, 4, kept, TILE), jnp.bfloat16),
            pltpu.VMEM((sizes[1] * sizes[2], 2, 2, kept, TILE), jnp.float32),
            pltpu.SemaphoreType.DMA((owners,)),
            pltpu.SemaphoreType.DMA((owners,)),
        ],
        compiler_params=pltpu.CompilerParams(
            collective_id=0, has_side_effects=True, vmem_limit_bytes=40 * 2**20
        ),
        name="exchange_and_columns",
    )(spec, jnp.asarray(w_high), jnp.asarray(w_low))


def twiddle_table(first, second, length):
    return (first * second % length).astype(jnp.float32) * (2.0 * math.pi / length)


def transform_columns(real_in, imag_in):
    lead, kept, length = real_in.shape
    outer = TILE
    inner = length // outer
    real_grid = real_in.reshape(lead, kept, outer, inner)
    imag_grid = imag_in.reshape(lead, kept, outer, inner)
    outer_pos = jnp.arange(outer, dtype=jnp.int32)
    inner_pos = jnp.arange(inner, dtype=jnp.int32)
    first_angle = twiddle_table(outer_pos[:, None], outer_pos[None, :], outer)
    first_cos = jnp.cos(first_angle)
    first_sin = jnp.sin(first_angle)
    section_real = jnp.einsum("ckab,ad->ckdb", real_grid, first_cos, precision=HIGH) + jnp.einsum(
        "ckab,ad->ckdb", imag_grid, first_sin, precision=HIGH
    )
    section_imag = jnp.einsum("ckab,ad->ckdb", imag_grid, first_cos, precision=HIGH) - jnp.einsum(
        "ckab,ad->ckdb", real_grid, first_sin, precision=HIGH
    )
    mid_angle = twiddle_table(outer_pos[:, None], inner_pos[None, :], length)
    mid_cos = jnp.cos(mid_angle)
    mid_sin = jnp.sin(mid_angle)
    turned_real = section_real * mid_cos + section_imag * mid_sin
    turned_imag = section_imag * mid_cos - section_real * mid_sin
    last_angle = twiddle_table(inner_pos[:, None], inner_pos[None, :], inner)
    last_cos = jnp.cos(last_angle)
    last_sin = jnp.sin(last_angle)
    final_real = jnp.einsum("ckdb,be->cked", turned_real, last_cos, precision=HIGH) + jnp.einsum(
        "ckdb,be->cked", turned_imag, last_sin, precision=HIGH
    )
    final_imag = jnp.einsum("ckdb,be->cked", turned_imag, last_cos, precision=HIGH) - jnp.einsum(
        "ckdb,be->cked", turned_real, last_sin, precision=HIGH
    )
    return (final_real.reshape(lead, kept, length), final_imag.reshape(lead, kept, length))


def exchange_many(spec, sizes):
    n_det, n_tm, n_pol = sizes
    owners = math.prod(sizes)
    kept = KY // owners
    half = kept // 2
    strips = n_tm * n_pol
    length = strips * TILE
    pieces = spec.reshape(2, 2, owners, 2, half, TILE)
    moved = lax.all_to_all(pieces, ("det", "tm", "pol"), split_axis=2, concat_axis=2, tiled=True)
    summed = jnp.sum(moved.reshape(2, 2, n_det, strips, 2, half, TILE).astype(jnp.float32), axis=2)
    columns = jnp.transpose(summed, (3, 1, 4, 0, 2, 5)).reshape(2, 2, kept, length)
    final_real, final_imag = transform_columns(columns[0], columns[1])
    norm_scale = 1.0 / math.sqrt(length * MAPY)
    real = final_real * norm_scale
    imag = final_imag * norm_scale
    position = (lax.axis_index("det") * n_tm + lax.axis_index("tm")) * n_pol + lax.axis_index("pol")
    cosine, sine = rotation(
        jnp.arange(length, dtype=jnp.int32)[None, :],
        length,
        (position * kept + jnp.arange(kept, dtype=jnp.int32))[:, None],
    )
    return (
        jnp.stack([cosine * real[0] + sine * real[1], cosine * imag[0] + sine * imag[1]]),
        jnp.stack([cosine * real[1] - sine * real[0], cosine * imag[1] - sine * imag[0]]),
    )


def solution(mesh):
    sizes = (mesh.shape["det"], mesh.shape["tm"], mesh.shape["pol"])
    owners = math.prod(sizes)

    def body(*args):
        spec = local_spectrum(*args, owners)
        if KY // owners % 16 == 0:
            return exchange(spec, sizes)
        return exchange_many(spec, sizes)

    in_specs = (
        P(("group", "det", "pol"), "tm"),
        P(("group", "tm")),
        P(("group", "det", "pol"), "tm"),
        P(("group", "det", "pol"), "tm"),
        P(("group", "det", "pol"), "tm"),
        P(("group", "det", "pol")),
        P(),
        P(("group", "det", "pol")),
    )
    out_specs = (
        P(None, ("group", "det", "tm", "pol"), None),
        P(None, ("group", "det", "tm", "pol"), None),
    )
    return jax.shard_map(body, mesh=mesh, in_specs=in_specs, out_specs=out_specs, check_vma=False)
```

```python
import math

import jax
import jax.numpy as jnp
import ml_dtypes
import numpy as np
from jax import lax
from jax.experimental import pallas as pl
from jax.experimental.pallas import tpu as pltpu
from jax.sharding import PartitionSpec as P

TILE = 128
MAPY = 2048
KY = 512
NANG = 8192
LANES = 128
CHUNK = 1024
HIGH = lax.Precision.HIGHEST
MESH = pl.DeviceIdType.MESH
NT = (((1,), (1,)), ((), ()))


def split_np(table):
    table = table.astype(np.float32)
    high = table.astype(ml_dtypes.bfloat16)
    low = (table - high.astype(np.float32)).astype(ml_dtypes.bfloat16)
    return high, low


def split(value):
    high = value.astype(jnp.bfloat16)
    return high, (value - high.astype(jnp.float32)).astype(jnp.bfloat16)


def row_tables(owners):
    kept = KY // owners
    ky = np.arange(KY).reshape(owners, 1, kept // 2, 2)
    ky = np.moveaxis(ky, 3, 0)
    y = np.arange(MAPY // 2)
    angle = (ky[..., None] * y % MAPY) * (2.0 * np.pi / MAPY)
    table = np.concatenate([np.cos(angle), -np.sin(angle)], axis=2)
    return split_np(table.reshape(2, KY, MAPY // 2))


def column_tables(length):
    pos = np.arange(length)
    angle = (pos[:, None] * pos[None, :] % length) * (2.0 * np.pi / length)
    table = np.concatenate([np.cos(angle), np.sin(angle)], axis=1)
    return split_np(table / math.sqrt(length * MAPY))


def rotation(kx, length, ky):
    fx = jnp.where(kx < length // 2, kx, kx - length).astype(jnp.float32)
    fy = ky.astype(jnp.float32)
    radius = jnp.maximum(fx * fx + fy * fy, 1.0)
    return (fx * fx - fy * fy) / radius, 2.0 * fx * fy / radius


def whole_kernel(
    sizes, direct,
    tile_ref, wafer_ref, angle_ref, ts_hbm, hwp_hbm, flags_hbm, pix_hbm, taps_hbm, thigh_hbm,
    tlow_hbm, *rest,
):
    n_det, n_tm, n_pol = sizes
    owners = n_det * n_tm * n_pol
    strips = n_tm * n_pol
    kept = KY // owners
    half = kept // 2
    length = strips * TILE
    if direct:
        whigh_hbm, wlow_hbm, e_ref, b_ref, *rest = rest
    else:
        out_ref, *rest = rest
    (ts, hwp_v, flags, pix, taps, t_high, t_low, in_sem, xs, cos_h, sin_h, q_s, u_s, rid_s, key_s,
     prev_s, last_s, sums_s, halo_send, halo_recv, *rest) = rest
    det_rows, time_len = ts.shape
    tap_count = taps.shape[1]
    width = (tap_count - 1) // 2
    block_count = tile_ref.shape[1]
    block_len = time_len // block_count
    tiles = MAPY // TILE
    det, tm, pol = lax.axis_index("det"), lax.axis_index("tm"), lax.axis_index("pol")
    me = (det * n_tm + tm) * n_pol + pol

    pairs = [(ts_hbm, ts), (hwp_hbm, hwp_v), (pix_hbm, pix), (taps_hbm, taps), (flags_hbm, flags),
             (thigh_hbm, t_high), (tlow_hbm, t_low)]
    if direct:
        w_high, w_low, spec_s, recv, ordered, send_sem, recv_sem = rest
        pairs += [(whigh_hbm, w_high), (wlow_hbm, w_low)]
    loads = [pltpu.make_async_copy(s, v, in_sem.at[i]) for i, (s, v) in enumerate(pairs)]
    for load in loads:
        load.start()

    xs[:, 0:LANES] = jnp.zeros((det_rows, LANES), jnp.float32)
    xs[:, LANES + time_len :] = jnp.zeros((det_rows, LANES), jnp.float32)
    barrier = pltpu.get_barrier_semaphore()
    has_left, has_right = tm > 0, tm < n_tm - 1
    if direct:
        order = [(s, x, c) for s in [2, 1, 3] + list(range(4, n_det)) if s < n_det
                 for x in range(n_tm) for c in range(n_pol)]
        order += [(0, x, c) for x in range(n_tm) for c in range(n_pol) if x or c]
        peers = [(lax.rem(det + s, n_det), lax.rem(tm + x, n_tm), lax.rem(pol + c, n_pol))
                 for s, x, c in order]
        for peer_det, peer_tm, peer_pol in peers:
            pl.semaphore_signal(
                barrier, inc=1, device_id={"det": peer_det, "tm": peer_tm, "pol": peer_pol},
                device_id_type=MESH,
            )
    else:
        @pl.when(has_left)
        def _():
            pl.semaphore_signal(barrier, inc=1, device_id={"tm": tm - 1}, device_id_type=MESH)

        @pl.when(has_right)
        def _():
            pl.semaphore_signal(barrier, inc=1, device_id={"tm": tm + 1}, device_id_type=MESH)

    def chain(b, last):
        last = list(last)
        for d in range(det_rows):
            tile = tile_ref[d, b]
            before = jnp.int32(0)
            for k in range(tiles):
                before = jnp.where(tile == k, last[k], before)
                last[k] = jnp.where(tile == k, b * det_rows + d + 1, last[k])
            prev_s[b * det_rows + d] = before
        return tuple(last)

    last = lax.fori_loop(0, block_count, chain, (jnp.int32(0),) * tiles)
    for k in range(tiles):
        last_s[k] = last[k]
    sums_s[0] = jnp.zeros(sums_s.shape[1:], jnp.float32)

    loads[0].wait()
    xs[:, LANES : LANES + time_len] = ts[...].astype(jnp.float32)
    if direct:
        pl.semaphore_wait(barrier, owners - 1)
    else:
        @pl.when(has_left)
        def _():
            pl.semaphore_wait(barrier, 1)

        @pl.when(has_right)
        def _():
            pl.semaphore_wait(barrier, 1)

    def halo(side):
        if side == 0:
            source, target, other = time_len, 0, lax.rem(tm + 1, n_tm)
        else:
            source, target, other = LANES, LANES + time_len, lax.rem(tm + n_tm - 1, n_tm)
        return pltpu.make_async_remote_copy(
            src_ref=xs.at[:, pl.ds(source, LANES)],
            dst_ref=xs.at[:, pl.ds(target, LANES)],
            send_sem=halo_send.at[side],
            recv_sem=halo_recv.at[side],
            device_id={"tm": other},
            device_id_type=MESH,
        )

    if n_tm > 1:
        @pl.when(has_right)
        def _():
            halo(0).start()

        @pl.when(has_left)
        def _():
            halo(1).start()

    loads[1].wait()
    hwp = (4 * hwp_v[...] % NANG).astype(jnp.float32) * (2.0 * math.pi / NANG)
    cos_h[...] = jnp.cos(hwp)
    sin_h[...] = jnp.sin(hwp)
    row = lax.broadcasted_iota(jnp.int32, (det_rows, LANES), 0)
    tap_row = lax.broadcasted_iota(jnp.int32, (det_rows, tap_count), 0)
    angle = jnp.zeros((det_rows, LANES), jnp.float32)
    wafer = jnp.zeros((det_rows, tap_count), jnp.int32)
    for d in range(det_rows):
        angle = jnp.where(row == d, angle_ref[d], angle)
        wafer = jnp.where(tap_row == d, wafer_ref[d], wafer)
    cos_a = jnp.cos(2.0 * angle)
    sin_a = jnp.sin(2.0 * angle)
    loads[2].wait()
    rid_s[...] = ((pix[...] >> 7) & (TILE // 2 - 1)).astype(jnp.float32)
    key_s[...] = (((pix[...] >> 13) << 7) + (pix[...] & (TILE - 1))).astype(jnp.float32)
    loads[3].wait()
    loads[4].wait()
    det_taps = jnp.zeros((det_rows, tap_count), jnp.float32)
    for w in range(taps.shape[0]):
        det_taps = det_taps + jnp.where(wafer == w, taps[w : w + 1, :], 0.0)

    chunk = min(CHUNK, time_len)
    chunks = time_len // chunk
    span = chunk + 2 * LANES
    per = chunk // LANES

    def filter_chunk(step):
        start = pl.multiple_of(step * chunk, chunk)
        base = xs[:, pl.ds(start, span)]
        total = jnp.zeros((det_rows, chunk), jnp.float32)
        for j in range(tap_count):
            moved = pltpu.roll(base, span - (LANES - width + j), 1)
            total = total + det_taps[:, j : j + 1] * moved[:, :chunk]
        flagged = total * flags[:, pl.ds(start, chunk)].astype(jnp.float32)
        rows = pl.ds(pl.multiple_of(step * per, per), per)
        ch = cos_h[rows, :]
        sh = sin_h[rows, :]
        for k in range(per):
            lanes = pl.ds(pl.multiple_of(start + k * LANES, LANES), LANES)
            part = flagged[:, k * LANES : (k + 1) * LANES]
            c = ch[k : k + 1, :]
            s = sh[k : k + 1, :]
            q_s[:, lanes] = part * (c * cos_a + s * sin_a)
            u_s[:, lanes] = part * (s * cos_a - c * sin_a)

    @pl.loop(1, chunks - 1)
    def _(step):
        filter_chunk(step)

    if n_tm > 1:
        @pl.when(has_left)
        def _():
            halo(0).wait_recv()
            halo(1).wait_send()

        @pl.when(has_right)
        def _():
            halo(1).wait_recv()
            halo(0).wait_send()

    @pl.loop(0, 2)
    def _(side):
        filter_chunk(side * (chunks - 1))

    sub = 16
    side = lax.broadcasted_iota(jnp.int32, (sub, block_len), 0).astype(jnp.float32)
    zero = jnp.zeros((sub, block_len), jnp.bfloat16)
    ids = [(side + float(g * sub)).astype(jnp.bfloat16) for g in range(TILE // 2 // sub)]
    lane = lax.broadcasted_iota(jnp.int32, (block_len, TILE), 1).astype(jnp.float32)
    keys = [lane.astype(jnp.bfloat16), (lane + float(TILE)).astype(jnp.bfloat16)]
    zeros = jnp.zeros((block_len, TILE), jnp.bfloat16)
    ones = jnp.ones((block_len, TILE), jnp.bfloat16)

    def spread(value):
        return jnp.broadcast_to(value, (sub, block_len)).astype(jnp.bfloat16)

    @pl.loop(0, block_count)
    def _(b):
        lanes = pl.ds(pl.multiple_of(b * block_len, block_len), block_len)
        turned = jnp.transpose(key_s[:, lanes])
        for d in range(det_rows):
            row_id = spread(rid_s[d : d + 1, lanes])
            qv = spread(q_s[d : d + 1, lanes])
            uv = spread(u_s[d : d + 1, lanes])
            hits = [row_id == i for i in ids]
            weighted = jnp.concatenate(
                [jnp.where(h, qv, zero) for h in hits] + [jnp.where(h, uv, zero) for h in hits],
                axis=0,
            )
            key = jnp.broadcast_to(turned[:, d : d + 1], (block_len, TILE)).astype(jnp.bfloat16)
            hot = jnp.concatenate([jnp.where(key == i, ones, zeros) for i in keys], axis=1)
            sums = jnp.dot(weighted, hot, preferred_element_type=jnp.float32)
            slot = b * det_rows + d
            sums_s[slot + 1] = sums_s[prev_s[slot]] + sums

    def tile_rows(k):
        found = sums_s[last_s[k]]
        return jnp.concatenate(
            [found[c * TILE // 2 : (c + 1) * TILE // 2, m * TILE : (m + 1) * TILE]
             for c in range(2) for m in range(2)], axis=0)

    first = jnp.concatenate([tile_rows(k) for k in range(tiles // 2)], axis=1)
    second = jnp.concatenate([tile_rows(k) for k in range(tiles // 2, tiles)], axis=1)
    for load in loads[5:]:
        load.wait()
    copies = [[], []]
    for parity in range(2):
        folded = first + second if parity == 0 else first - second
        f_high, f_low = split(folded)
        acc = lax.dot_general(t_high[parity], f_high, NT, preferred_element_type=jnp.float32)
        acc = acc + lax.dot_general(t_high[parity], f_low, NT, preferred_element_type=jnp.float32)
        acc = acc + lax.dot_general(t_low[parity], f_high, NT, preferred_element_type=jnp.float32)
        for c in range(2):
            piece = acc[:, c * TILE : (c + 1) * TILE].astype(jnp.bfloat16)
            if direct:
                spec_s[parity, c] = piece
            else:
                out_ref[2 * parity + c] = piece
        if not direct:
            continue
        for at, (peer_det, peer_tm, peer_pol) in enumerate(peers):
            peer = (peer_det * n_tm + peer_tm) * n_pol + peer_pol
            copy = pltpu.make_async_remote_copy(
                src_ref=spec_s.at[parity, :, pl.ds(pl.multiple_of(peer * kept, kept), kept), :],
                dst_ref=recv.at[me, parity],
                send_sem=send_sem.at[parity, at],
                recv_sem=recv_sem.at[parity, at],
                device_id={"det": peer_det, "tm": peer_tm, "pol": peer_pol},
                device_id_type=MESH,
            )
            copy.start()
            copies[parity].append(copy)
    if not direct:
        return

    own = pl.ds(pl.multiple_of(me * kept, kept), kept)
    for parity in range(2):
        recv[me, parity] = spec_s[parity, :, own, :]
    kx = lax.broadcasted_iota(jnp.int32, (kept, length), 1)
    ky = me * kept + lax.broadcasted_iota(jnp.int32, (kept, length), 0)
    cosine, sine = rotation(kx, length, ky)
    for parity in range(2):
        for copy in copies[parity]:
            copy.wait_recv()
        for strip in range(strips):
            total = recv[strip, parity].astype(jnp.float32)
            for d in range(1, n_det):
                total = total + recv[d * strips + strip, parity].astype(jnp.float32)
            for c in range(2):
                for part in range(2):
                    ordered[strip, c, part, pl.ds(parity, half, stride=2), :] = total[
                        c, part * half : (part + 1) * half
                    ]
    columns = [ordered[strip].reshape(4 * kept, TILE) for strip in range(strips)]
    x_high, x_low = split(jnp.concatenate(columns, axis=1))
    acc = jnp.dot(x_high, w_high[...], preferred_element_type=jnp.float32)
    acc = acc + jnp.dot(x_low, w_high[...], preferred_element_type=jnp.float32)
    acc = acc + jnp.dot(x_high, w_low[...], preferred_element_type=jnp.float32)
    real, imag = [], []
    for c in range(2):
        re_rows = slice(2 * c * kept, (2 * c + 1) * kept)
        im_rows = slice((2 * c + 1) * kept, (2 * c + 2) * kept)
        real.append(acc[re_rows, :length] + acc[im_rows, length:])
        imag.append(acc[im_rows, :length] - acc[re_rows, length:])
    e_ref[0] = cosine * real[0] + sine * real[1]
    e_ref[1] = cosine * imag[0] + sine * imag[1]
    b_ref[0] = cosine * real[1] - sine * real[0]
    b_ref[1] = cosine * imag[1] - sine * imag[0]
    for parity in range(2):
        for copy in copies[parity]:
            copy.wait_send()


def run_whole(sizes, direct, timestream, hwp_index, flags, pixel_index, tile_index, wafer, taps, angle):
    det_rows, time_len = timestream.shape
    owners = math.prod(sizes)
    strips = sizes[1] * sizes[2]
    kept = KY // owners
    length = strips * TILE
    blocks = tile_index.size
    tables = [jnp.asarray(t) for t in row_tables(owners)]
    if direct:
        tables += [jnp.asarray(t) for t in column_tables(length)]
    hwp_grid = hwp_index.reshape(time_len // LANES, LANES)
    loaded = [timestream, hwp_grid, flags, pixel_index, taps] + tables[:2]
    smem = pl.BlockSpec(memory_space=pltpu.SMEM)
    vmem = pl.BlockSpec(memory_space=pltpu.VMEM)
    hbm = pl.BlockSpec(memory_space=pl.ANY)
    wide = pltpu.VMEM((det_rows, time_len), jnp.float32)
    grid = pltpu.VMEM((time_len // LANES, LANES), jnp.float32)
    scratch = [pltpu.VMEM(x.shape, x.dtype) for x in loaded]
    scratch += [
        pltpu.SemaphoreType.DMA((9,)),
        pltpu.VMEM((det_rows, time_len + 2 * LANES), jnp.float32),
        grid, grid, wide, wide, wide, wide,
        pltpu.SMEM((blocks,), jnp.int32),
        pltpu.SMEM((MAPY // TILE,), jnp.int32),
        pltpu.VMEM((blocks + 1, TILE, 2 * TILE), jnp.float32),
        pltpu.SemaphoreType.DMA((2,)),
        pltpu.SemaphoreType.DMA((2,)),
    ]
    if direct:
        scratch += [pltpu.VMEM(x.shape, x.dtype) for x in tables[2:]]
        scratch += [
            pltpu.VMEM((2, 2, KY, TILE), jnp.bfloat16),
            pltpu.VMEM((owners, 2, 2, kept, TILE), jnp.bfloat16),
            pltpu.VMEM((strips, 2, 2, kept, TILE), jnp.float32),
            pltpu.SemaphoreType.DMA((2, owners)),
            pltpu.SemaphoreType.DMA((2, owners)),
        ]
        shape = jax.ShapeDtypeStruct((2, kept, length), jnp.float32)
        out_shape, out_specs = (shape, shape), (vmem, vmem)
    else:
        out_shape, out_specs = jax.ShapeDtypeStruct((4, KY, TILE), jnp.bfloat16), vmem

    def kernel(*refs):
        whole_kernel(sizes, direct, *refs)

    return pl.pallas_call(
        kernel,
        out_shape=out_shape,
        in_specs=[smem] * 3 + [hbm] * (5 + len(tables)),
        out_specs=out_specs,
        scratch_shapes=scratch,
        compiler_params=pltpu.CompilerParams(
            collective_id=0, has_side_effects=True, vmem_limit_bytes=56 * 2**20
        ),
        name="map_to_modes",
    )(tile_index, wafer, angle, timestream, hwp_grid, flags, pixel_index, taps, *tables)


def twiddle_table(first, second, length):
    return (first * second % length).astype(jnp.float32) * (2.0 * math.pi / length)


def transform_columns(real_in, imag_in):
    lead, kept, length = real_in.shape
    outer = TILE
    inner = length // outer
    real_grid = real_in.reshape(lead, kept, outer, inner)
    imag_grid = imag_in.reshape(lead, kept, outer, inner)
    outer_pos = jnp.arange(outer, dtype=jnp.int32)
    inner_pos = jnp.arange(inner, dtype=jnp.int32)
    first_angle = twiddle_table(outer_pos[:, None], outer_pos[None, :], outer)
    first_cos = jnp.cos(first_angle)
    first_sin = jnp.sin(first_angle)
    section_real = jnp.einsum("ckab,ad->ckdb", real_grid, first_cos, precision=HIGH) + jnp.einsum(
        "ckab,ad->ckdb", imag_grid, first_sin, precision=HIGH
    )
    section_imag = jnp.einsum("ckab,ad->ckdb", imag_grid, first_cos, precision=HIGH) - jnp.einsum(
        "ckab,ad->ckdb", real_grid, first_sin, precision=HIGH
    )
    mid_angle = twiddle_table(outer_pos[:, None], inner_pos[None, :], length)
    mid_cos = jnp.cos(mid_angle)
    mid_sin = jnp.sin(mid_angle)
    turned_real = section_real * mid_cos + section_imag * mid_sin
    turned_imag = section_imag * mid_cos - section_real * mid_sin
    last_angle = twiddle_table(inner_pos[:, None], inner_pos[None, :], inner)
    last_cos = jnp.cos(last_angle)
    last_sin = jnp.sin(last_angle)
    final_real = jnp.einsum("ckdb,be->cked", turned_real, last_cos, precision=HIGH) + jnp.einsum(
        "ckdb,be->cked", turned_imag, last_sin, precision=HIGH
    )
    final_imag = jnp.einsum("ckdb,be->cked", turned_imag, last_cos, precision=HIGH) - jnp.einsum(
        "ckdb,be->cked", turned_real, last_sin, precision=HIGH
    )
    return (final_real.reshape(lead, kept, length), final_imag.reshape(lead, kept, length))


def exchange_many(spec, sizes):
    n_det, n_tm, n_pol = sizes
    owners = math.prod(sizes)
    kept = KY // owners
    half = kept // 2
    strips = n_tm * n_pol
    length = strips * TILE
    pieces = spec.reshape(2, 2, owners, 2, half, TILE)
    moved = lax.all_to_all(pieces, ("det", "tm", "pol"), split_axis=2, concat_axis=2, tiled=True)
    summed = jnp.sum(moved.reshape(2, 2, n_det, strips, 2, half, TILE).astype(jnp.float32), axis=2)
    columns = jnp.transpose(summed, (3, 1, 4, 0, 2, 5)).reshape(2, 2, kept, length)
    final_real, final_imag = transform_columns(columns[0], columns[1])
    norm_scale = 1.0 / math.sqrt(length * MAPY)
    real = final_real * norm_scale
    imag = final_imag * norm_scale
    position = (lax.axis_index("det") * n_tm + lax.axis_index("tm")) * n_pol + lax.axis_index("pol")
    cosine, sine = rotation(
        jnp.arange(length, dtype=jnp.int32)[None, :],
        length,
        (position * kept + jnp.arange(kept, dtype=jnp.int32))[:, None],
    )
    return (
        jnp.stack([cosine * real[0] + sine * real[1], cosine * imag[0] + sine * imag[1]]),
        jnp.stack([cosine * real[1] - sine * real[0], cosine * imag[1] - sine * imag[0]]),
    )


def solution(mesh):
    sizes = (mesh.shape["det"], mesh.shape["tm"], mesh.shape["pol"])
    direct = KY // math.prod(sizes) % 32 == 0

    def body(*args):
        found = run_whole(sizes, direct, *args)
        return found if direct else exchange_many(found, sizes)

    in_specs = (
        P(("group", "det", "pol"), "tm"),
        P(("group", "tm")),
        P(("group", "det", "pol"), "tm"),
        P(("group", "det", "pol"), "tm"),
        P(("group", "det", "pol"), "tm"),
        P(("group", "det", "pol")),
        P(),
        P(("group", "det", "pol")),
    )
    out_specs = (
        P(None, ("group", "det", "tm", "pol"), None),
        P(None, ("group", "det", "tm", "pol"), None),
    )
    return jax.shard_map(body, mesh=mesh, in_specs=in_specs, out_specs=out_specs, check_vma=False)
```

```python
import math

import jax
import jax.numpy as jnp
import ml_dtypes
import numpy as np
from jax import lax
from jax.experimental import pallas as pl
from jax.experimental.pallas import tpu as pltpu
from jax.sharding import PartitionSpec as P

TILE = 128
MAPY = 2048
KY = 512
NANG = 8192
LANES = 128
CHUNK = 1024
HIGH = lax.Precision.HIGHEST
MESH = pl.DeviceIdType.MESH
NT = (((1,), (1,)), ((), ()))


def split_np(table):
    table = table.astype(np.float32)
    high = table.astype(ml_dtypes.bfloat16)
    low = (table - high.astype(np.float32)).astype(ml_dtypes.bfloat16)
    return high, low


def split(value):
    high = value.astype(jnp.bfloat16)
    return high, (value - high.astype(jnp.float32)).astype(jnp.bfloat16)


def row_tables(owners):
    kept = KY // owners
    ky = np.arange(KY).reshape(owners, 1, kept // 2, 2)
    ky = np.moveaxis(ky, 3, 0)
    y = np.arange(MAPY // 2)
    angle = (ky[..., None] * y % MAPY) * (2.0 * np.pi / MAPY)
    table = np.concatenate([np.cos(angle), -np.sin(angle)], axis=2)
    return split_np(table.reshape(2, KY, MAPY // 2))


def column_tables(length):
    pos = np.arange(length)
    angle = (pos[:, None] * pos[None, :] % length) * (2.0 * np.pi / length)
    table = np.concatenate([np.cos(angle), np.sin(angle)], axis=1)
    return split_np(table / math.sqrt(length * MAPY))


def rotation(kx, length, ky):
    fx = jnp.where(kx < length // 2, kx, kx - length).astype(jnp.float32)
    fy = ky.astype(jnp.float32)
    radius = jnp.maximum(fx * fx + fy * fy, 1.0)
    return (fx * fx - fy * fy) / radius, 2.0 * fx * fy / radius


def whole_kernel(
    sizes, direct,
    tile_ref, wafer_ref, angle_ref, ts_hbm, hwp_hbm, flags_hbm, pix_hbm, taps_hbm, thigh_hbm,
    tlow_hbm, *rest,
):
    n_det, n_tm, n_pol = sizes
    owners = n_det * n_tm * n_pol
    strips = n_tm * n_pol
    kept = KY // owners
    half = kept // 2
    length = strips * TILE
    if direct:
        whigh_hbm, wlow_hbm, modes_ref, *rest = rest
    else:
        out_ref, *rest = rest
    (ts, hwp_v, flags, pix, taps, t_high, t_low, in_sem, xs, cos_h, sin_h, q_s, u_s, rid_s, key_s,
     prev_s, last_s, sums_s, halo_send, halo_recv, *rest) = rest
    det_rows, time_len = ts.shape
    tap_count = taps.shape[1]
    width = (tap_count - 1) // 2
    block_count = tile_ref.shape[1]
    block_len = time_len // block_count
    tiles = MAPY // TILE
    det, tm, pol = lax.axis_index("det"), lax.axis_index("tm"), lax.axis_index("pol")
    me = (det * n_tm + tm) * n_pol + pol

    pairs = [(ts_hbm, ts), (hwp_hbm, hwp_v), (pix_hbm, pix), (taps_hbm, taps), (flags_hbm, flags),
             (thigh_hbm, t_high), (tlow_hbm, t_low)]
    if direct:
        w_high, w_low, spec_s, recv, passed, joined, ordered, send_sem, recv_sem, chunk_send, chunk_recv = rest
        pairs += [(whigh_hbm, w_high), (wlow_hbm, w_low)]
    loads = [pltpu.make_async_copy(s, v, in_sem.at[i]) for i, (s, v) in enumerate(pairs)]
    for load in loads:
        load.start()

    xs[:, 0:LANES] = jnp.zeros((det_rows, LANES), jnp.float32)
    xs[:, LANES + time_len :] = jnp.zeros((det_rows, LANES), jnp.float32)
    barrier = pltpu.get_barrier_semaphore()
    has_left, has_right = tm > 0, tm < n_tm - 1
    if direct:
        turns = [(lax.rem(tm + x, n_tm), lax.rem(pol + c, n_pol))
                 for x in range(n_tm) for c in range(n_pol)]
        for s in range(n_det):
            for r, (peer_tm, peer_pol) in enumerate(turns):
                if s or r:
                    peer = {"det": lax.rem(det + s, n_det), "tm": peer_tm, "pol": peer_pol}
                    pl.semaphore_signal(barrier, inc=1, device_id=peer, device_id_type=MESH)
    else:
        @pl.when(has_left)
        def _():
            pl.semaphore_signal(barrier, inc=1, device_id={"tm": tm - 1}, device_id_type=MESH)

        @pl.when(has_right)
        def _():
            pl.semaphore_signal(barrier, inc=1, device_id={"tm": tm + 1}, device_id_type=MESH)

    def chain(b, last):
        last = list(last)
        for d in range(det_rows):
            tile = tile_ref[d, b]
            before = jnp.int32(0)
            for k in range(tiles):
                before = jnp.where(tile == k, last[k], before)
                last[k] = jnp.where(tile == k, b * det_rows + d + 1, last[k])
            prev_s[b * det_rows + d] = before
        return tuple(last)

    last = lax.fori_loop(0, block_count, chain, (jnp.int32(0),) * tiles)
    for k in range(tiles):
        last_s[k] = last[k]
    sums_s[0] = jnp.zeros(sums_s.shape[1:], jnp.float32)

    loads[0].wait()
    xs[:, LANES : LANES + time_len] = ts[...].astype(jnp.float32)
    if direct:
        pl.semaphore_wait(barrier, owners - 1)
    else:
        @pl.when(has_left)
        def _():
            pl.semaphore_wait(barrier, 1)

        @pl.when(has_right)
        def _():
            pl.semaphore_wait(barrier, 1)

    def halo(side):
        if side == 0:
            source, target, other = time_len, 0, lax.rem(tm + 1, n_tm)
        else:
            source, target, other = LANES, LANES + time_len, lax.rem(tm + n_tm - 1, n_tm)
        return pltpu.make_async_remote_copy(
            src_ref=xs.at[:, pl.ds(source, LANES)],
            dst_ref=xs.at[:, pl.ds(target, LANES)],
            send_sem=halo_send.at[side],
            recv_sem=halo_recv.at[side],
            device_id={"tm": other},
            device_id_type=MESH,
        )

    if n_tm > 1:
        @pl.when(has_right)
        def _():
            halo(0).start()

        @pl.when(has_left)
        def _():
            halo(1).start()

    loads[1].wait()
    hwp = (4 * hwp_v[...] % NANG).astype(jnp.float32) * (2.0 * math.pi / NANG)
    cos_h[...] = jnp.cos(hwp)
    sin_h[...] = jnp.sin(hwp)
    row = lax.broadcasted_iota(jnp.int32, (det_rows, LANES), 0)
    tap_row = lax.broadcasted_iota(jnp.int32, (det_rows, tap_count), 0)
    angle = jnp.zeros((det_rows, LANES), jnp.float32)
    wafer = jnp.zeros((det_rows, tap_count), jnp.int32)
    for d in range(det_rows):
        angle = jnp.where(row == d, angle_ref[d], angle)
        wafer = jnp.where(tap_row == d, wafer_ref[d], wafer)
    cos_a = jnp.cos(2.0 * angle)
    sin_a = jnp.sin(2.0 * angle)
    loads[2].wait()
    rid_s[...] = ((pix[...] >> 7) & (TILE // 2 - 1)).astype(jnp.float32)
    key_s[...] = (((pix[...] >> 13) << 7) + (pix[...] & (TILE - 1))).astype(jnp.float32)
    loads[3].wait()
    loads[4].wait()
    det_taps = jnp.zeros((det_rows, tap_count), jnp.float32)
    for w in range(taps.shape[0]):
        det_taps = det_taps + jnp.where(wafer == w, taps[w : w + 1, :], 0.0)

    chunk = min(CHUNK, time_len)
    chunks = time_len // chunk
    span = chunk + 2 * LANES
    per = chunk // LANES

    def filter_chunk(step):
        start = pl.multiple_of(step * chunk, chunk)
        base = xs[:, pl.ds(start, span)]
        total = jnp.zeros((det_rows, chunk), jnp.float32)
        for j in range(tap_count):
            moved = pltpu.roll(base, span - (LANES - width + j), 1)
            total = total + det_taps[:, j : j + 1] * moved[:, :chunk]
        flagged = total * flags[:, pl.ds(start, chunk)].astype(jnp.float32)
        rows = pl.ds(pl.multiple_of(step * per, per), per)
        ch = cos_h[rows, :]
        sh = sin_h[rows, :]
        for k in range(per):
            lanes = pl.ds(pl.multiple_of(start + k * LANES, LANES), LANES)
            part = flagged[:, k * LANES : (k + 1) * LANES]
            c = ch[k : k + 1, :]
            s = sh[k : k + 1, :]
            q_s[:, lanes] = part * (c * cos_a + s * sin_a)
            u_s[:, lanes] = part * (s * cos_a - c * sin_a)

    @pl.loop(1, chunks - 1)
    def _(step):
        filter_chunk(step)

    if n_tm > 1:
        @pl.when(has_left)
        def _():
            halo(0).wait_recv()
            halo(1).wait_send()

        @pl.when(has_right)
        def _():
            halo(1).wait_recv()
            halo(0).wait_send()

    @pl.loop(0, 2)
    def _(side):
        filter_chunk(side * (chunks - 1))

    sub = 16
    side = lax.broadcasted_iota(jnp.int32, (sub, block_len), 0).astype(jnp.float32)
    zero = jnp.zeros((sub, block_len), jnp.bfloat16)
    ids = [(side + float(g * sub)).astype(jnp.bfloat16) for g in range(TILE // 2 // sub)]
    lane = lax.broadcasted_iota(jnp.int32, (block_len, TILE), 1).astype(jnp.float32)
    keys = [lane.astype(jnp.bfloat16), (lane + float(TILE)).astype(jnp.bfloat16)]
    zeros = jnp.zeros((block_len, TILE), jnp.bfloat16)
    ones = jnp.ones((block_len, TILE), jnp.bfloat16)

    def spread(value):
        return jnp.broadcast_to(value, (sub, block_len)).astype(jnp.bfloat16)

    @pl.loop(0, block_count)
    def _(b):
        lanes = pl.ds(pl.multiple_of(b * block_len, block_len), block_len)
        turned = jnp.transpose(key_s[:, lanes])
        for d in range(det_rows):
            row_id = spread(rid_s[d : d + 1, lanes])
            qv = spread(q_s[d : d + 1, lanes])
            uv = spread(u_s[d : d + 1, lanes])
            hits = [row_id == i for i in ids]
            weighted = jnp.concatenate(
                [jnp.where(h, qv, zero) for h in hits] + [jnp.where(h, uv, zero) for h in hits],
                axis=0,
            )
            key = jnp.broadcast_to(turned[:, d : d + 1], (block_len, TILE)).astype(jnp.bfloat16)
            hot = jnp.concatenate([jnp.where(key == i, ones, zeros) for i in keys], axis=1)
            sums = jnp.dot(weighted, hot, preferred_element_type=jnp.float32)
            slot = b * det_rows + d
            sums_s[slot + 1] = sums_s[prev_s[slot]] + sums

    def tile_rows(k):
        found = sums_s[last_s[k]]
        return jnp.concatenate(
            [found[c * TILE // 2 : (c + 1) * TILE // 2, m * TILE : (m + 1) * TILE]
             for c in range(2) for m in range(2)], axis=0)

    first = jnp.concatenate([tile_rows(k) for k in range(tiles // 2)], axis=1)
    second = jnp.concatenate([tile_rows(k) for k in range(tiles // 2, tiles)], axis=1)
    for load in loads[5:]:
        load.wait()
    if direct:
        strip_at = tm * n_pol + pol
        near = det // 2 * 2 + 1 - lax.rem(det, 2)
        left = det < 2
        edge = (det == 0) | (det == n_det - 1)
        inner = (det == 1) | (det == 2)
        far = [jnp.where(left, 3 - h, h) for h in range(2)]

        def piece_rows(peer_det, r):
            peer = (peer_det * n_tm + turns[r][0]) * n_pol + turns[r][1]
            return pl.ds(pl.multiple_of(peer * kept, kept), kept)

        def send(kind, r, parity, h=0):
            peer_det = (det, near, far[h])[kind]
            if kind < 2:
                source = spec_s.at[parity, :, piece_rows(peer_det, r), :]
            else:
                peer = turns[r][0] * n_pol + turns[r][1]
                source = joined.at[parity, h, :, pl.ds(pl.multiple_of(peer * kept, kept), kept), :]
            return pltpu.make_async_remote_copy(
                src_ref=source,
                dst_ref=recv.at[kind, strip_at, parity],
                send_sem=send_sem.at[kind + h, r, parity],
                recv_sem=recv_sem.at[kind, r, parity],
                device_id={"det": peer_det, "tm": turns[r][0], "pol": turns[r][1]},
                device_id_type=MESH,
            )

        def send_chunk(parity, h):
            rows = pl.ds(pl.multiple_of(far[h] * strips * kept, strips * kept), strips * kept)
            return pltpu.make_async_remote_copy(
                src_ref=spec_s.at[parity, :, rows, :],
                dst_ref=passed.at[parity, h],
                send_sem=chunk_send.at[parity, h],
                recv_sem=chunk_recv.at[parity, h],
                device_id={"det": near},
                device_id_type=MESH,
            )

        def send_near(parity):
            for r in range(strips):
                send(1, r, parity).start()
            for r in range(1, strips):
                send(0, r, parity).start()

    for parity in range(2):
        folded = first + second if parity == 0 else first - second
        f_high, f_low = split(folded)
        acc = lax.dot_general(t_high[parity], f_high, NT, preferred_element_type=jnp.float32)
        acc = acc + lax.dot_general(t_high[parity], f_low, NT, preferred_element_type=jnp.float32)
        acc = acc + lax.dot_general(t_low[parity], f_high, NT, preferred_element_type=jnp.float32)
        for c in range(2):
            piece = acc[:, c * TILE : (c + 1) * TILE].astype(jnp.bfloat16)
            if direct:
                spec_s[parity, c] = piece
            else:
                out_ref[2 * parity + c] = piece
        if direct:
            @pl.when(edge)
            def _():
                for h in range(2):
                    send_chunk(parity, h).start()

            @pl.when(inner)
            def _():
                send_near(parity)
    if not direct:
        return

    @pl.when(edge)
    def _():
        for parity in range(2):
            send_near(parity)

    @pl.when(inner)
    def _():
        for parity in range(2):
            for h in range(2):
                send_chunk(parity, h).wait_recv()
                rows = pl.ds(pl.multiple_of(far[h] * strips * kept, strips * kept), strips * kept)
                both = passed[parity, h].astype(jnp.float32) + spec_s[parity, :, rows, :].astype(
                    jnp.float32
                )
                joined[parity, h] = both.astype(jnp.bfloat16)
                for r in range(strips):
                    send(2, r, parity, h).start()

    own = pl.ds(pl.multiple_of(me * kept, kept), kept)
    for parity in range(2):
        recv[0, strip_at, parity] = spec_s[parity, :, own, :]
    for parity in range(2):
        for kind in range(3):
            for r in range(0 if kind else 1, strips):
                send(kind, r, parity).wait_recv()
        for strip in range(strips):
            total = recv[0, strip, parity].astype(jnp.float32)
            for kind in range(1, 3):
                total = total + recv[kind, strip, parity].astype(jnp.float32)
            for c in range(2):
                for part in range(2):
                    ordered[strip, c, part, pl.ds(parity, half, stride=2), :] = total[
                        c, part * half : (part + 1) * half
                    ]
    columns = [ordered[strip].reshape(4 * kept, TILE) for strip in range(strips)]
    x_high, x_low = split(jnp.concatenate(columns, axis=1))
    acc = jnp.dot(x_high, w_high[...], preferred_element_type=jnp.float32)
    acc = acc + jnp.dot(x_low, w_high[...], preferred_element_type=jnp.float32)
    acc = acc + jnp.dot(x_high, w_low[...], preferred_element_type=jnp.float32)
    real, imag = [], []
    for c in range(2):
        re_rows = slice(2 * c * kept, (2 * c + 1) * kept)
        im_rows = slice((2 * c + 1) * kept, (2 * c + 2) * kept)
        real.append(acc[re_rows, :length] + acc[im_rows, length:])
        imag.append(acc[im_rows, :length] - acc[re_rows, length:])
    for c in range(2):
        modes_ref[c, 0] = real[c]
        modes_ref[c, 1] = imag[c]
    for parity in range(2):
        for kind in range(2):
            for r in range(0 if kind else 1, strips):
                send(kind, r, parity).wait_send()

    @pl.when(edge)
    def _():
        for parity in range(2):
            for h in range(2):
                send_chunk(parity, h).wait_send()

    @pl.when(inner)
    def _():
        for parity in range(2):
            for h in range(2):
                for r in range(strips):
                    send(2, r, parity, h).wait_send()


def run_whole(sizes, direct, timestream, hwp_index, flags, pixel_index, tile_index, wafer, taps, angle):
    det_rows, time_len = timestream.shape
    owners = math.prod(sizes)
    strips = sizes[1] * sizes[2]
    kept = KY // owners
    length = strips * TILE
    blocks = tile_index.size
    tables = [jnp.asarray(t) for t in row_tables(owners)]
    if direct:
        tables += [jnp.asarray(t) for t in column_tables(length)]
    hwp_grid = hwp_index.reshape(time_len // LANES, LANES)
    loaded = [timestream, hwp_grid, flags, pixel_index, taps] + tables[:2]
    smem = pl.BlockSpec(memory_space=pltpu.SMEM)
    vmem = pl.BlockSpec(memory_space=pltpu.VMEM)
    hbm = pl.BlockSpec(memory_space=pl.ANY)
    wide = pltpu.VMEM((det_rows, time_len), jnp.float32)
    grid = pltpu.VMEM((time_len // LANES, LANES), jnp.float32)
    scratch = [pltpu.VMEM(x.shape, x.dtype) for x in loaded]
    scratch += [
        pltpu.SemaphoreType.DMA((9,)),
        pltpu.VMEM((det_rows, time_len + 2 * LANES), jnp.float32),
        grid, grid, wide, wide, wide, wide,
        pltpu.SMEM((blocks,), jnp.int32),
        pltpu.SMEM((MAPY // TILE,), jnp.int32),
        pltpu.VMEM((blocks + 1, TILE, 2 * TILE), jnp.float32),
        pltpu.SemaphoreType.DMA((2,)),
        pltpu.SemaphoreType.DMA((2,)),
    ]
    if direct:
        scratch += [pltpu.VMEM(x.shape, x.dtype) for x in tables[2:]]
        scratch += [
            pltpu.VMEM((2, 2, KY, TILE), jnp.bfloat16),
            pltpu.VMEM((3, strips, 2, 2, kept, TILE), jnp.bfloat16),
            pltpu.VMEM((2, 2, 2, strips * kept, TILE), jnp.bfloat16),
            pltpu.VMEM((2, 2, 2, strips * kept, TILE), jnp.bfloat16),
            pltpu.VMEM((strips, 2, 2, kept, TILE), jnp.float32),
            pltpu.SemaphoreType.DMA((4, strips, 2)),
            pltpu.SemaphoreType.DMA((3, strips, 2)),
            pltpu.SemaphoreType.DMA((2, 2)),
            pltpu.SemaphoreType.DMA((2, 2)),
        ]
        out_shape, out_specs = jax.ShapeDtypeStruct((2, 2, kept, length), jnp.float32), vmem
    else:
        out_shape, out_specs = jax.ShapeDtypeStruct((4, KY, TILE), jnp.bfloat16), vmem

    def kernel(*refs):
        whole_kernel(sizes, direct, *refs)

    return pl.pallas_call(
        kernel,
        out_shape=out_shape,
        in_specs=[smem] * 3 + [hbm] * (5 + len(tables)),
        out_specs=out_specs,
        scratch_shapes=scratch,
        compiler_params=pltpu.CompilerParams(
            collective_id=0, has_side_effects=True, vmem_limit_bytes=56 * 2**20
        ),
        name="map_to_modes",
    )(tile_index, wafer, angle, timestream, hwp_grid, flags, pixel_index, taps, *tables)


def twiddle_table(first, second, length):
    return (first * second % length).astype(jnp.float32) * (2.0 * math.pi / length)


def transform_columns(real_in, imag_in):
    lead, kept, length = real_in.shape
    outer = TILE
    inner = length // outer
    real_grid = real_in.reshape(lead, kept, outer, inner)
    imag_grid = imag_in.reshape(lead, kept, outer, inner)
    outer_pos = jnp.arange(outer, dtype=jnp.int32)
    inner_pos = jnp.arange(inner, dtype=jnp.int32)
    first_angle = twiddle_table(outer_pos[:, None], outer_pos[None, :], outer)
    first_cos = jnp.cos(first_angle)
    first_sin = jnp.sin(first_angle)
    section_real = jnp.einsum("ckab,ad->ckdb", real_grid, first_cos, precision=HIGH) + jnp.einsum(
        "ckab,ad->ckdb", imag_grid, first_sin, precision=HIGH
    )
    section_imag = jnp.einsum("ckab,ad->ckdb", imag_grid, first_cos, precision=HIGH) - jnp.einsum(
        "ckab,ad->ckdb", real_grid, first_sin, precision=HIGH
    )
    mid_angle = twiddle_table(outer_pos[:, None], inner_pos[None, :], length)
    mid_cos = jnp.cos(mid_angle)
    mid_sin = jnp.sin(mid_angle)
    turned_real = section_real * mid_cos + section_imag * mid_sin
    turned_imag = section_imag * mid_cos - section_real * mid_sin
    last_angle = twiddle_table(inner_pos[:, None], inner_pos[None, :], inner)
    last_cos = jnp.cos(last_angle)
    last_sin = jnp.sin(last_angle)
    final_real = jnp.einsum("ckdb,be->cked", turned_real, last_cos, precision=HIGH) + jnp.einsum(
        "ckdb,be->cked", turned_imag, last_sin, precision=HIGH
    )
    final_imag = jnp.einsum("ckdb,be->cked", turned_imag, last_cos, precision=HIGH) - jnp.einsum(
        "ckdb,be->cked", turned_real, last_sin, precision=HIGH
    )
    return (final_real.reshape(lead, kept, length), final_imag.reshape(lead, kept, length))


def exchange_many(spec, sizes):
    n_det, n_tm, n_pol = sizes
    owners = math.prod(sizes)
    kept = KY // owners
    half = kept // 2
    strips = n_tm * n_pol
    length = strips * TILE
    pieces = spec.reshape(2, 2, owners, 2, half, TILE)
    moved = lax.all_to_all(pieces, ("det", "tm", "pol"), split_axis=2, concat_axis=2, tiled=True)
    summed = jnp.sum(moved.reshape(2, 2, n_det, strips, 2, half, TILE).astype(jnp.float32), axis=2)
    columns = jnp.transpose(summed, (3, 1, 4, 0, 2, 5)).reshape(2, 2, kept, length)
    final_real, final_imag = transform_columns(columns[0], columns[1])
    norm_scale = 1.0 / math.sqrt(length * MAPY)
    real = final_real * norm_scale
    imag = final_imag * norm_scale
    position = (lax.axis_index("det") * n_tm + lax.axis_index("tm")) * n_pol + lax.axis_index("pol")
    cosine, sine = rotation(
        jnp.arange(length, dtype=jnp.int32)[None, :],
        length,
        (position * kept + jnp.arange(kept, dtype=jnp.int32))[:, None],
    )
    return (
        jnp.stack([cosine * real[0] + sine * real[1], cosine * imag[0] + sine * imag[1]]),
        jnp.stack([cosine * real[1] - sine * real[0], cosine * imag[1] - sine * imag[0]]),
    )


def solution(mesh):
    sizes = (mesh.shape["det"], mesh.shape["tm"], mesh.shape["pol"])
    direct = sizes[0] == 4 and KY // math.prod(sizes) % 32 == 0

    def body(*args):
        found = run_whole(sizes, direct, *args)
        if not direct:
            return exchange_many(found, sizes)
        _, _, kept, length = found.shape
        at = (lax.axis_index("det") * sizes[1] + lax.axis_index("tm")) * sizes[2]
        at = (at + lax.axis_index("pol")) * kept
        shape = (2, kept, length)
        kx = lax.broadcasted_iota(jnp.int32, shape, 2)
        cosine, sine = rotation(kx, length, at + lax.broadcasted_iota(jnp.int32, shape, 1))
        return cosine * found[0] + sine * found[1], cosine * found[1] - sine * found[0]

    in_specs = (
        P(("group", "det", "pol"), "tm"),
        P(("group", "tm")),
        P(("group", "det", "pol"), "tm"),
        P(("group", "det", "pol"), "tm"),
        P(("group", "det", "pol"), "tm"),
        P(("group", "det", "pol")),
        P(),
        P(("group", "det", "pol")),
    )
    out_specs = (
        P(None, ("group", "det", "tm", "pol"), None),
        P(None, ("group", "det", "tm", "pol"), None),
    )
    return jax.shard_map(body, mesh=mesh, in_specs=in_specs, out_specs=out_specs, check_vma=False)
```

```python
import math

import jax
import jax.numpy as jnp
import ml_dtypes
import numpy as np
from jax import lax
from jax.experimental import pallas as pl
from jax.experimental.pallas import tpu as pltpu
from jax.sharding import PartitionSpec as P

TILE = 128
MAPY = 2048
KY = 512
NANG = 8192
LANES = 128
CHUNK = 1024
HIGH = lax.Precision.HIGHEST
MESH = pl.DeviceIdType.MESH
NT = (((1,), (1,)), ((), ()))


def split_np(table):
    table = table.astype(np.float32)
    high = table.astype(ml_dtypes.bfloat16)
    low = (table - high.astype(np.float32)).astype(ml_dtypes.bfloat16)
    return high, low


def split(value):
    high = value.astype(jnp.bfloat16)
    return high, (value - high.astype(jnp.float32)).astype(jnp.bfloat16)


def row_tables(owners):
    kept = KY // owners
    ky = np.arange(KY).reshape(owners, 1, kept // 2, 2)
    ky = np.moveaxis(ky, 3, 0)
    y = np.arange(MAPY // 2)
    angle = (ky[..., None] * y % MAPY) * (2.0 * np.pi / MAPY)
    table = np.concatenate([np.cos(angle), -np.sin(angle)], axis=2)
    return split_np(table.reshape(2, KY, MAPY // 2))


def column_tables(length):
    pos = np.arange(length)
    angle = (pos[:, None] * pos[None, :] % length) * (2.0 * np.pi / length)
    table = np.concatenate([np.cos(angle), np.sin(angle)], axis=1)
    return split_np(table / math.sqrt(length * MAPY))


def rotation(kx, length, ky):
    fx = jnp.where(kx < length // 2, kx, kx - length).astype(jnp.float32)
    fy = ky.astype(jnp.float32)
    radius = jnp.maximum(fx * fx + fy * fy, 1.0)
    return (fx * fx - fy * fy) / radius, 2.0 * fx * fy / radius


def whole_kernel(
    sizes, direct,
    tile_ref, wafer_ref, angle_ref, ts_hbm, hwp_hbm, flags_hbm, pix_hbm, taps_hbm, thigh_hbm,
    tlow_hbm, *rest,
):
    n_det, n_tm, n_pol = sizes
    owners = n_det * n_tm * n_pol
    strips = n_tm * n_pol
    kept = KY // owners
    half = kept // 2
    length = strips * TILE
    if direct:
        whigh_hbm, wlow_hbm, modes_ref, *rest = rest
    else:
        out_ref, *rest = rest
    (ts, hwp_v, flags, pix, taps, t_high, t_low, in_sem, xs, cos_h, sin_h, q_s, u_s, rid_s, key_s,
     prev_s, last_s, sums_s, halo_send, halo_recv, *rest) = rest
    det_rows, time_len = ts.shape
    tap_count = taps.shape[1]
    width = (tap_count - 1) // 2
    block_count = tile_ref.shape[1]
    block_len = time_len // block_count
    tiles = MAPY // TILE
    det, tm, pol = lax.axis_index("det"), lax.axis_index("tm"), lax.axis_index("pol")
    me = (det * n_tm + tm) * n_pol + pol

    pairs = [(ts_hbm, ts), (hwp_hbm, hwp_v), (pix_hbm, pix), (taps_hbm, taps), (flags_hbm, flags),
             (thigh_hbm, t_high), (tlow_hbm, t_low)]
    if direct:
        w_high, w_low, spec_s, recv, passed, joined, ordered, send_sem, recv_sem, chunk_send, chunk_recv = rest
        pairs += [(whigh_hbm, w_high), (wlow_hbm, w_low)]
    loads = [pltpu.make_async_copy(s, v, in_sem.at[i]) for i, (s, v) in enumerate(pairs)]
    for load in loads:
        load.start()

    xs[:, 0:LANES] = jnp.zeros((det_rows, LANES), jnp.float32)
    xs[:, LANES + time_len :] = jnp.zeros((det_rows, LANES), jnp.float32)
    barrier = pltpu.get_barrier_semaphore()
    has_left, has_right = tm > 0, tm < n_tm - 1
    if direct:
        turns = [(lax.rem(tm + x, n_tm), lax.rem(pol + c, n_pol))
                 for x in range(n_tm) for c in range(n_pol)]
        for s in range(n_det):
            for r, (peer_tm, peer_pol) in enumerate(turns):
                if s or r:
                    peer = {"det": lax.rem(det + s, n_det), "tm": peer_tm, "pol": peer_pol}
                    pl.semaphore_signal(barrier, inc=1, device_id=peer, device_id_type=MESH)
    else:
        @pl.when(has_left)
        def _():
            pl.semaphore_signal(barrier, inc=1, device_id={"tm": tm - 1}, device_id_type=MESH)

        @pl.when(has_right)
        def _():
            pl.semaphore_signal(barrier, inc=1, device_id={"tm": tm + 1}, device_id_type=MESH)

    def chain(b, last):
        last = list(last)
        for d in range(det_rows):
            tile = tile_ref[d, b]
            before = jnp.int32(0)
            for k in range(tiles):
                before = jnp.where(tile == k, last[k], before)
                last[k] = jnp.where(tile == k, b * det_rows + d + 1, last[k])
            prev_s[b * det_rows + d] = before
        return tuple(last)

    last = lax.fori_loop(0, block_count, chain, (jnp.int32(0),) * tiles)
    for k in range(tiles):
        last_s[k] = last[k]
    sums_s[0] = jnp.zeros(sums_s.shape[1:], jnp.float32)

    loads[0].wait()
    xs[:, LANES : LANES + time_len] = ts[...].astype(jnp.float32)
    if direct:
        pl.semaphore_wait(barrier, owners - 1)
    else:
        @pl.when(has_left)
        def _():
            pl.semaphore_wait(barrier, 1)

        @pl.when(has_right)
        def _():
            pl.semaphore_wait(barrier, 1)

    def halo(side):
        if side == 0:
            source, target, other = time_len, 0, lax.rem(tm + 1, n_tm)
        else:
            source, target, other = LANES, LANES + time_len, lax.rem(tm + n_tm - 1, n_tm)
        return pltpu.make_async_remote_copy(
            src_ref=xs.at[:, pl.ds(source, LANES)],
            dst_ref=xs.at[:, pl.ds(target, LANES)],
            send_sem=halo_send.at[side],
            recv_sem=halo_recv.at[side],
            device_id={"tm": other},
            device_id_type=MESH,
        )

    if n_tm > 1:
        @pl.when(has_right)
        def _():
            halo(0).start()

        @pl.when(has_left)
        def _():
            halo(1).start()

    loads[1].wait()
    hwp = (4 * hwp_v[...] % NANG).astype(jnp.float32) * (2.0 * math.pi / NANG)
    cos_h[...] = jnp.cos(hwp)
    sin_h[...] = jnp.sin(hwp)
    row = lax.broadcasted_iota(jnp.int32, (det_rows, LANES), 0)
    tap_row = lax.broadcasted_iota(jnp.int32, (det_rows, tap_count), 0)
    angle = jnp.zeros((det_rows, LANES), jnp.float32)
    wafer = jnp.zeros((det_rows, tap_count), jnp.int32)
    for d in range(det_rows):
        angle = jnp.where(row == d, angle_ref[d], angle)
        wafer = jnp.where(tap_row == d, wafer_ref[d], wafer)
    cos_a = jnp.cos(2.0 * angle)
    sin_a = jnp.sin(2.0 * angle)
    loads[2].wait()
    rid_s[...] = ((pix[...] >> 7) & (TILE // 2 - 1)).astype(jnp.float32)
    key_s[...] = (((pix[...] >> 13) << 7) + (pix[...] & (TILE - 1))).astype(jnp.float32)
    loads[3].wait()
    loads[4].wait()
    det_taps = jnp.zeros((det_rows, tap_count), jnp.float32)
    for w in range(taps.shape[0]):
        det_taps = det_taps + jnp.where(wafer == w, taps[w : w + 1, :], 0.0)

    chunk = min(CHUNK, time_len)
    chunks = time_len // chunk
    span = chunk + 2 * LANES
    per = chunk // LANES

    def filter_chunk(step):
        start = pl.multiple_of(step * chunk, chunk)
        base = xs[:, pl.ds(start, span)]
        total = jnp.zeros((det_rows, chunk), jnp.float32)
        for j in range(tap_count):
            moved = pltpu.roll(base, span - (LANES - width + j), 1)
            total = total + det_taps[:, j : j + 1] * moved[:, :chunk]
        flagged = total * flags[:, pl.ds(start, chunk)].astype(jnp.float32)
        rows = pl.ds(pl.multiple_of(step * per, per), per)
        ch = cos_h[rows, :]
        sh = sin_h[rows, :]
        for k in range(per):
            lanes = pl.ds(pl.multiple_of(start + k * LANES, LANES), LANES)
            part = flagged[:, k * LANES : (k + 1) * LANES]
            c = ch[k : k + 1, :]
            s = sh[k : k + 1, :]
            q_s[:, lanes] = part * (c * cos_a + s * sin_a)
            u_s[:, lanes] = part * (s * cos_a - c * sin_a)

    @pl.loop(1, chunks - 1)
    def _(step):
        filter_chunk(step)

    if n_tm > 1:
        @pl.when(has_left)
        def _():
            halo(0).wait_recv()
            halo(1).wait_send()

        @pl.when(has_right)
        def _():
            halo(1).wait_recv()
            halo(0).wait_send()

    @pl.loop(0, 2)
    def _(side):
        filter_chunk(side * (chunks - 1))

    sub = 16
    side = lax.broadcasted_iota(jnp.int32, (sub, block_len), 0).astype(jnp.float32)
    zero = jnp.zeros((sub, block_len), jnp.bfloat16)
    ids = [(side + float(g * sub)).astype(jnp.bfloat16) for g in range(TILE // 2 // sub)]
    lane = lax.broadcasted_iota(jnp.int32, (block_len, TILE), 1).astype(jnp.float32)
    keys = [lane.astype(jnp.bfloat16), (lane + float(TILE)).astype(jnp.bfloat16)]
    zeros = jnp.zeros((block_len, TILE), jnp.bfloat16)
    ones = jnp.ones((block_len, TILE), jnp.bfloat16)

    def spread(value):
        return jnp.broadcast_to(value, (sub, block_len)).astype(jnp.bfloat16)

    @pl.loop(0, block_count)
    def _(b):
        lanes = pl.ds(pl.multiple_of(b * block_len, block_len), block_len)
        turned = jnp.transpose(key_s[:, lanes])
        for d in range(det_rows):
            row_id = spread(rid_s[d : d + 1, lanes])
            qv = spread(q_s[d : d + 1, lanes])
            uv = spread(u_s[d : d + 1, lanes])
            hits = [row_id == i for i in ids]
            weighted = jnp.concatenate(
                [jnp.where(h, qv, zero) for h in hits] + [jnp.where(h, uv, zero) for h in hits],
                axis=0,
            )
            key = jnp.broadcast_to(turned[:, d : d + 1], (block_len, TILE)).astype(jnp.bfloat16)
            hot = jnp.concatenate([jnp.where(key == i, ones, zeros) for i in keys], axis=1)
            sums = jnp.dot(weighted, hot, preferred_element_type=jnp.float32)
            slot = b * det_rows + d
            sums_s[slot + 1] = sums_s[prev_s[slot]] + sums

    def tile_rows(k):
        found = sums_s[last_s[k]]
        return jnp.concatenate(
            [found[c * TILE // 2 : (c + 1) * TILE // 2, m * TILE : (m + 1) * TILE]
             for c in range(2) for m in range(2)], axis=0)

    first = jnp.concatenate([tile_rows(k) for k in range(tiles // 2)], axis=1)
    second = jnp.concatenate([tile_rows(k) for k in range(tiles // 2, tiles)], axis=1)
    for load in loads[5:]:
        load.wait()
    if direct:
        strip_at = tm * n_pol + pol
        near = det // 2 * 2 + 1 - lax.rem(det, 2)
        left = det < 2
        edge = (det == 0) | (det == n_det - 1)
        inner = (det == 1) | (det == 2)
        far = [jnp.where(left, 3 - h, h) for h in range(2)]

        def piece_rows(peer_det, r):
            peer = (peer_det * n_tm + turns[r][0]) * n_pol + turns[r][1]
            return pl.ds(pl.multiple_of(peer * kept, kept), kept)

        def send(kind, r, parity, h=0):
            peer_det = (det, near, far[h])[kind]
            if kind < 2:
                source = spec_s.at[parity, :, piece_rows(peer_det, r), :]
            else:
                peer = turns[r][0] * n_pol + turns[r][1]
                source = joined.at[parity, h, :, pl.ds(pl.multiple_of(peer * kept, kept), kept), :]
            return pltpu.make_async_remote_copy(
                src_ref=source,
                dst_ref=recv.at[kind, strip_at, parity],
                send_sem=send_sem.at[kind + h, r, parity],
                recv_sem=recv_sem.at[kind, r, parity],
                device_id={"det": peer_det, "tm": turns[r][0], "pol": turns[r][1]},
                device_id_type=MESH,
            )

        def send_chunk(parity, h):
            rows = pl.ds(pl.multiple_of(far[h] * strips * kept, strips * kept), strips * kept)
            return pltpu.make_async_remote_copy(
                src_ref=spec_s.at[parity, :, rows, :],
                dst_ref=passed.at[parity, h],
                send_sem=chunk_send.at[parity, h],
                recv_sem=chunk_recv.at[parity, h],
                device_id={"det": near},
                device_id_type=MESH,
            )

        def send_near(parity):
            for r in range(strips):
                send(1, r, parity).start()
            for r in range(1, strips):
                send(0, r, parity).start()

    folds = [split(first + second), split(first - second)]
    starts = [jnp.where(left, KY // 2, 0), jnp.where(left, 0, KY // 2)] if direct else [0]
    count = KY // len(starts)
    for at, start in enumerate(starts):
        rows = pl.ds(pl.multiple_of(start, count), count)
        for parity, (f_high, f_low) in enumerate(folds):
            table = t_high[parity, rows, :]
            acc = lax.dot_general(table, f_high, NT, preferred_element_type=jnp.float32)
            acc = acc + lax.dot_general(table, f_low, NT, preferred_element_type=jnp.float32)
            acc = acc + lax.dot_general(
                t_low[parity, rows, :], f_high, NT, preferred_element_type=jnp.float32
            )
            for c in range(2):
                piece = acc[:, c * TILE : (c + 1) * TILE].astype(jnp.bfloat16)
                if direct:
                    spec_s[parity, c, rows, :] = piece
                else:
                    out_ref[2 * parity + c] = piece
            if direct and at:
                send_near(parity)
            elif direct:
                @pl.when(edge)
                def _():
                    for h in range(2):
                        send_chunk(parity, h).start()
    if not direct:
        return

    @pl.when(inner)
    def _():
        for parity in range(2):
            for h in range(2):
                send_chunk(parity, h).wait_recv()
                rows = pl.ds(pl.multiple_of(far[h] * strips * kept, strips * kept), strips * kept)
                both = passed[parity, h].astype(jnp.float32) + spec_s[parity, :, rows, :].astype(
                    jnp.float32
                )
                joined[parity, h] = both.astype(jnp.bfloat16)
                for r in range(strips):
                    send(2, r, parity, h).start()

    own = pl.ds(pl.multiple_of(me * kept, kept), kept)
    for parity in range(2):
        recv[0, strip_at, parity] = spec_s[parity, :, own, :]
    for parity in range(2):
        for kind in range(3):
            for r in range(0 if kind else 1, strips):
                send(kind, r, parity).wait_recv()
        for strip in range(strips):
            total = recv[0, strip, parity].astype(jnp.float32)
            for kind in range(1, 3):
                total = total + recv[kind, strip, parity].astype(jnp.float32)
            for c in range(2):
                for part in range(2):
                    ordered[strip, c, part, pl.ds(parity, half, stride=2), :] = total[
                        c, part * half : (part + 1) * half
                    ]
    columns = [ordered[strip].reshape(4 * kept, TILE) for strip in range(strips)]
    x_high, x_low = split(jnp.concatenate(columns, axis=1))
    acc = jnp.dot(x_high, w_high[...], preferred_element_type=jnp.float32)
    acc = acc + jnp.dot(x_low, w_high[...], preferred_element_type=jnp.float32)
    acc = acc + jnp.dot(x_high, w_low[...], preferred_element_type=jnp.float32)
    real, imag = [], []
    for c in range(2):
        re_rows = slice(2 * c * kept, (2 * c + 1) * kept)
        im_rows = slice((2 * c + 1) * kept, (2 * c + 2) * kept)
        real.append(acc[re_rows, :length] + acc[im_rows, length:])
        imag.append(acc[im_rows, :length] - acc[re_rows, length:])
    for c in range(2):
        modes_ref[c, 0] = real[c]
        modes_ref[c, 1] = imag[c]
    for parity in range(2):
        for kind in range(2):
            for r in range(0 if kind else 1, strips):
                send(kind, r, parity).wait_send()

    @pl.when(edge)
    def _():
        for parity in range(2):
            for h in range(2):
                send_chunk(parity, h).wait_send()

    @pl.when(inner)
    def _():
        for parity in range(2):
            for h in range(2):
                for r in range(strips):
                    send(2, r, parity, h).wait_send()


def run_whole(sizes, direct, timestream, hwp_index, flags, pixel_index, tile_index, wafer, taps, angle):
    det_rows, time_len = timestream.shape
    owners = math.prod(sizes)
    strips = sizes[1] * sizes[2]
    kept = KY // owners
    length = strips * TILE
    blocks = tile_index.size
    tables = [jnp.asarray(t) for t in row_tables(owners)]
    if direct:
        tables += [jnp.asarray(t) for t in column_tables(length)]
    hwp_grid = hwp_index.reshape(time_len // LANES, LANES)
    loaded = [timestream, hwp_grid, flags, pixel_index, taps] + tables[:2]
    smem = pl.BlockSpec(memory_space=pltpu.SMEM)
    vmem = pl.BlockSpec(memory_space=pltpu.VMEM)
    hbm = pl.BlockSpec(memory_space=pl.ANY)
    wide = pltpu.VMEM((det_rows, time_len), jnp.float32)
    grid = pltpu.VMEM((time_len // LANES, LANES), jnp.float32)
    scratch = [pltpu.VMEM(x.shape, x.dtype) for x in loaded]
    scratch += [
        pltpu.SemaphoreType.DMA((9,)),
        pltpu.VMEM((det_rows, time_len + 2 * LANES), jnp.float32),
        grid, grid, wide, wide, wide, wide,
        pltpu.SMEM((blocks,), jnp.int32),
        pltpu.SMEM((MAPY // TILE,), jnp.int32),
        pltpu.VMEM((blocks + 1, TILE, 2 * TILE), jnp.float32),
        pltpu.SemaphoreType.DMA((2,)),
        pltpu.SemaphoreType.DMA((2,)),
    ]
    if direct:
        scratch += [pltpu.VMEM(x.shape, x.dtype) for x in tables[2:]]
        scratch += [
            pltpu.VMEM((2, 2, KY, TILE), jnp.bfloat16),
            pltpu.VMEM((3, strips, 2, 2, kept, TILE), jnp.bfloat16),
            pltpu.VMEM((2, 2, 2, strips * kept, TILE), jnp.bfloat16),
            pltpu.VMEM((2, 2, 2, strips * kept, TILE), jnp.bfloat16),
            pltpu.VMEM((strips, 2, 2, kept, TILE), jnp.float32),
            pltpu.SemaphoreType.DMA((4, strips, 2)),
            pltpu.SemaphoreType.DMA((3, strips, 2)),
            pltpu.SemaphoreType.DMA((2, 2)),
            pltpu.SemaphoreType.DMA((2, 2)),
        ]
        out_shape, out_specs = jax.ShapeDtypeStruct((2, 2, kept, length), jnp.float32), vmem
    else:
        out_shape, out_specs = jax.ShapeDtypeStruct((4, KY, TILE), jnp.bfloat16), vmem

    def kernel(*refs):
        whole_kernel(sizes, direct, *refs)

    return pl.pallas_call(
        kernel,
        out_shape=out_shape,
        in_specs=[smem] * 3 + [hbm] * (5 + len(tables)),
        out_specs=out_specs,
        scratch_shapes=scratch,
        compiler_params=pltpu.CompilerParams(
            collective_id=0, has_side_effects=True, vmem_limit_bytes=56 * 2**20
        ),
        name="map_to_modes",
    )(tile_index, wafer, angle, timestream, hwp_grid, flags, pixel_index, taps, *tables)


def twiddle_table(first, second, length):
    return (first * second % length).astype(jnp.float32) * (2.0 * math.pi / length)


def transform_columns(real_in, imag_in):
    lead, kept, length = real_in.shape
    outer = TILE
    inner = length // outer
    real_grid = real_in.reshape(lead, kept, outer, inner)
    imag_grid = imag_in.reshape(lead, kept, outer, inner)
    outer_pos = jnp.arange(outer, dtype=jnp.int32)
    inner_pos = jnp.arange(inner, dtype=jnp.int32)
    first_angle = twiddle_table(outer_pos[:, None], outer_pos[None, :], outer)
    first_cos = jnp.cos(first_angle)
    first_sin = jnp.sin(first_angle)
    section_real = jnp.einsum("ckab,ad->ckdb", real_grid, first_cos, precision=HIGH) + jnp.einsum(
        "ckab,ad->ckdb", imag_grid, first_sin, precision=HIGH
    )
    section_imag = jnp.einsum("ckab,ad->ckdb", imag_grid, first_cos, precision=HIGH) - jnp.einsum(
        "ckab,ad->ckdb", real_grid, first_sin, precision=HIGH
    )
    mid_angle = twiddle_table(outer_pos[:, None], inner_pos[None, :], length)
    mid_cos = jnp.cos(mid_angle)
    mid_sin = jnp.sin(mid_angle)
    turned_real = section_real * mid_cos + section_imag * mid_sin
    turned_imag = section_imag * mid_cos - section_real * mid_sin
    last_angle = twiddle_table(inner_pos[:, None], inner_pos[None, :], inner)
    last_cos = jnp.cos(last_angle)
    last_sin = jnp.sin(last_angle)
    final_real = jnp.einsum("ckdb,be->cked", turned_real, last_cos, precision=HIGH) + jnp.einsum(
        "ckdb,be->cked", turned_imag, last_sin, precision=HIGH
    )
    final_imag = jnp.einsum("ckdb,be->cked", turned_imag, last_cos, precision=HIGH) - jnp.einsum(
        "ckdb,be->cked", turned_real, last_sin, precision=HIGH
    )
    return (final_real.reshape(lead, kept, length), final_imag.reshape(lead, kept, length))


def exchange_many(spec, sizes):
    n_det, n_tm, n_pol = sizes
    owners = math.prod(sizes)
    kept = KY // owners
    half = kept // 2
    strips = n_tm * n_pol
    length = strips * TILE
    pieces = spec.reshape(2, 2, owners, 2, half, TILE)
    moved = lax.all_to_all(pieces, ("det", "tm", "pol"), split_axis=2, concat_axis=2, tiled=True)
    summed = jnp.sum(moved.reshape(2, 2, n_det, strips, 2, half, TILE).astype(jnp.float32), axis=2)
    columns = jnp.transpose(summed, (3, 1, 4, 0, 2, 5)).reshape(2, 2, kept, length)
    final_real, final_imag = transform_columns(columns[0], columns[1])
    norm_scale = 1.0 / math.sqrt(length * MAPY)
    real = final_real * norm_scale
    imag = final_imag * norm_scale
    position = (lax.axis_index("det") * n_tm + lax.axis_index("tm")) * n_pol + lax.axis_index("pol")
    cosine, sine = rotation(
        jnp.arange(length, dtype=jnp.int32)[None, :],
        length,
        (position * kept + jnp.arange(kept, dtype=jnp.int32))[:, None],
    )
    return (
        jnp.stack([cosine * real[0] + sine * real[1], cosine * imag[0] + sine * imag[1]]),
        jnp.stack([cosine * real[1] - sine * real[0], cosine * imag[1] - sine * imag[0]]),
    )


def solution(mesh):
    sizes = (mesh.shape["det"], mesh.shape["tm"], mesh.shape["pol"])
    direct = sizes[0] == 4 and KY // math.prod(sizes) % 32 == 0

    def body(*args):
        found = run_whole(sizes, direct, *args)
        if not direct:
            return exchange_many(found, sizes)
        _, _, kept, length = found.shape
        at = (lax.axis_index("det") * sizes[1] + lax.axis_index("tm")) * sizes[2]
        at = (at + lax.axis_index("pol")) * kept
        shape = (2, kept, length)
        kx = lax.broadcasted_iota(jnp.int32, shape, 2)
        cosine, sine = rotation(kx, length, at + lax.broadcasted_iota(jnp.int32, shape, 1))
        return cosine * found[0] + sine * found[1], cosine * found[1] - sine * found[0]

    in_specs = (
        P(("group", "det", "pol"), "tm"),
        P(("group", "tm")),
        P(("group", "det", "pol"), "tm"),
        P(("group", "det", "pol"), "tm"),
        P(("group", "det", "pol"), "tm"),
        P(("group", "det", "pol")),
        P(),
        P(("group", "det", "pol")),
    )
    out_specs = (
        P(None, ("group", "det", "tm", "pol"), None),
        P(None, ("group", "det", "tm", "pol"), None),
    )
    return jax.shard_map(body, mesh=mesh, in_specs=in_specs, out_specs=out_specs, check_vma=False)
```

```python
import math

import jax
import jax.numpy as jnp
import ml_dtypes
import numpy as np
from jax import lax
from jax.experimental import pallas as pl
from jax.experimental.pallas import tpu as pltpu
from jax.sharding import PartitionSpec as P

TILE = 128
MAPY = 2048
KY = 512
NANG = 8192
LANES = 128
CHUNK = 1024
HIGH = lax.Precision.HIGHEST
MESH = pl.DeviceIdType.MESH
NT = (((1,), (1,)), ((), ()))


def split_np(table):
    table = table.astype(np.float32)
    high = table.astype(ml_dtypes.bfloat16)
    low = (table - high.astype(np.float32)).astype(ml_dtypes.bfloat16)
    return high, low


def split(value):
    high = value.astype(jnp.bfloat16)
    return high, (value - high.astype(jnp.float32)).astype(jnp.bfloat16)


def row_tables(owners):
    kept = KY // owners
    ky = np.arange(KY).reshape(owners, 1, kept // 2, 2)
    ky = np.moveaxis(ky, 3, 0)
    y = np.arange(MAPY // 2)
    angle = (ky[..., None] * y % MAPY) * (2.0 * np.pi / MAPY)
    table = np.concatenate([np.cos(angle), -np.sin(angle)], axis=2)
    return split_np(table.reshape(2, KY, MAPY // 2))


def column_tables(length):
    pos = np.arange(length)
    angle = (pos[:, None] * pos[None, :] % length) * (2.0 * np.pi / length)
    table = np.concatenate([np.cos(angle), np.sin(angle)], axis=1)
    return split_np(table / math.sqrt(length * MAPY))


def rotation(kx, length, ky):
    fx = jnp.where(kx < length // 2, kx, kx - length).astype(jnp.float32)
    fy = ky.astype(jnp.float32)
    radius = jnp.maximum(fx * fx + fy * fy, 1.0)
    return (fx * fx - fy * fy) / radius, 2.0 * fx * fy / radius


def whole_kernel(
    sizes, direct,
    tile_ref, wafer_ref, angle_ref, ts_hbm, hwp_hbm, flags_hbm, pix_hbm, taps_hbm, thigh_hbm,
    tlow_hbm, *rest,
):
    n_det, n_tm, n_pol = sizes
    owners = n_det * n_tm * n_pol
    strips = n_tm * n_pol
    kept = KY // owners
    half = kept // 2
    length = strips * TILE
    if direct:
        whigh_hbm, wlow_hbm, modes_ref, *rest = rest
    else:
        out_ref, *rest = rest
    (ts, hwp_v, flags, pix, taps, t_high, t_low, in_sem, xs, cos_h, sin_h, q_s, u_s, rid_s, key_s,
     prev_s, last_s, sums_s, halo_send, halo_recv, *rest) = rest
    det_rows, time_len = ts.shape
    tap_count = taps.shape[1]
    width = (tap_count - 1) // 2
    block_count = tile_ref.shape[1]
    block_len = time_len // block_count
    tiles = MAPY // TILE
    det, tm, pol = lax.axis_index("det"), lax.axis_index("tm"), lax.axis_index("pol")
    me = (det * n_tm + tm) * n_pol + pol

    pairs = [(ts_hbm, ts), (hwp_hbm, hwp_v), (pix_hbm, pix), (taps_hbm, taps), (flags_hbm, flags),
             (thigh_hbm, t_high), (tlow_hbm, t_low)]
    if direct:
        w_high, w_low, spec_s, recv, passed, joined, ordered, send_sem, recv_sem, chunk_send, chunk_recv = rest
        pairs += [(whigh_hbm, w_high), (wlow_hbm, w_low)]
    loads = [pltpu.make_async_copy(s, v, in_sem.at[i]) for i, (s, v) in enumerate(pairs)]
    for load in loads:
        load.start()

    xs[:, 0:LANES] = jnp.zeros((det_rows, LANES), jnp.float32)
    xs[:, LANES + time_len :] = jnp.zeros((det_rows, LANES), jnp.float32)
    barrier = pltpu.get_barrier_semaphore()
    has_left, has_right = tm > 0, tm < n_tm - 1
    if direct:
        turns = [(lax.rem(tm + x, n_tm), lax.rem(pol + c, n_pol))
                 for x in range(n_tm) for c in range(n_pol)]
        for s in range(n_det):
            for r, (peer_tm, peer_pol) in enumerate(turns):
                if s or r:
                    peer = {"det": lax.rem(det + s, n_det), "tm": peer_tm, "pol": peer_pol}
                    pl.semaphore_signal(barrier, inc=1, device_id=peer, device_id_type=MESH)
    else:
        @pl.when(has_left)
        def _():
            pl.semaphore_signal(barrier, inc=1, device_id={"tm": tm - 1}, device_id_type=MESH)

        @pl.when(has_right)
        def _():
            pl.semaphore_signal(barrier, inc=1, device_id={"tm": tm + 1}, device_id_type=MESH)

    def chain(b, last):
        last = list(last)
        for d in range(det_rows):
            tile = tile_ref[d, b]
            before = jnp.int32(0)
            for k in range(tiles):
                before = jnp.where(tile == k, last[k], before)
                last[k] = jnp.where(tile == k, b * det_rows + d + 1, last[k])
            prev_s[b * det_rows + d] = before
        return tuple(last)

    last = lax.fori_loop(0, block_count, chain, (jnp.int32(0),) * tiles)
    for k in range(tiles):
        last_s[k] = last[k]
    sums_s[0] = jnp.zeros(sums_s.shape[1:], jnp.float32)

    loads[0].wait()
    xs[:, LANES : LANES + time_len] = ts[...].astype(jnp.float32)
    if direct:
        pl.semaphore_wait(barrier, owners - 1)
    else:
        @pl.when(has_left)
        def _():
            pl.semaphore_wait(barrier, 1)

        @pl.when(has_right)
        def _():
            pl.semaphore_wait(barrier, 1)

    def halo(side):
        if side == 0:
            source, target, other = time_len, 0, lax.rem(tm + 1, n_tm)
        else:
            source, target, other = LANES, LANES + time_len, lax.rem(tm + n_tm - 1, n_tm)
        return pltpu.make_async_remote_copy(
            src_ref=xs.at[:, pl.ds(source, LANES)],
            dst_ref=xs.at[:, pl.ds(target, LANES)],
            send_sem=halo_send.at[side],
            recv_sem=halo_recv.at[side],
            device_id={"tm": other},
            device_id_type=MESH,
        )

    if n_tm > 1:
        @pl.when(has_right)
        def _():
            halo(0).start()

        @pl.when(has_left)
        def _():
            halo(1).start()

    loads[1].wait()
    hwp = (4 * hwp_v[...] % NANG).astype(jnp.float32) * (2.0 * math.pi / NANG)
    cos_h[...] = jnp.cos(hwp)
    sin_h[...] = jnp.sin(hwp)
    row = lax.broadcasted_iota(jnp.int32, (det_rows, LANES), 0)
    tap_row = lax.broadcasted_iota(jnp.int32, (det_rows, tap_count), 0)
    angle = jnp.zeros((det_rows, LANES), jnp.float32)
    wafer = jnp.zeros((det_rows, tap_count), jnp.int32)
    for d in range(det_rows):
        angle = jnp.where(row == d, angle_ref[d], angle)
        wafer = jnp.where(tap_row == d, wafer_ref[d], wafer)
    cos_a = jnp.cos(2.0 * angle)
    sin_a = jnp.sin(2.0 * angle)
    loads[2].wait()
    rid_s[...] = ((pix[...] >> 7) & (TILE // 2 - 1)).astype(jnp.float32)
    key_s[...] = (((pix[...] >> 13) << 7) + (pix[...] & (TILE - 1))).astype(jnp.float32)
    loads[3].wait()
    loads[4].wait()
    det_taps = jnp.zeros((det_rows, tap_count), jnp.float32)
    for w in range(taps.shape[0]):
        det_taps = det_taps + jnp.where(wafer == w, taps[w : w + 1, :], 0.0)

    chunk = min(CHUNK, time_len)
    chunks = time_len // chunk
    span = chunk + 2 * LANES
    per = chunk // LANES

    def filter_chunk(step):
        start = pl.multiple_of(step * chunk, chunk)
        base = xs[:, pl.ds(start, span)]
        total = jnp.zeros((det_rows, chunk), jnp.float32)
        for j in range(tap_count):
            moved = pltpu.roll(base, span - (LANES - width + j), 1)
            total = total + det_taps[:, j : j + 1] * moved[:, :chunk]
        flagged = total * flags[:, pl.ds(start, chunk)].astype(jnp.float32)
        rows = pl.ds(pl.multiple_of(step * per, per), per)
        ch = cos_h[rows, :]
        sh = sin_h[rows, :]
        for k in range(per):
            lanes = pl.ds(pl.multiple_of(start + k * LANES, LANES), LANES)
            part = flagged[:, k * LANES : (k + 1) * LANES]
            c = ch[k : k + 1, :]
            s = sh[k : k + 1, :]
            q_s[:, lanes] = part * (c * cos_a + s * sin_a)
            u_s[:, lanes] = part * (s * cos_a - c * sin_a)

    @pl.loop(1, chunks - 1)
    def _(step):
        filter_chunk(step)

    if n_tm > 1:
        @pl.when(has_left)
        def _():
            halo(0).wait_recv()
            halo(1).wait_send()

        @pl.when(has_right)
        def _():
            halo(1).wait_recv()
            halo(0).wait_send()

    @pl.loop(0, 2)
    def _(side):
        filter_chunk(side * (chunks - 1))

    sub = 16
    side = lax.broadcasted_iota(jnp.int32, (sub, block_len), 0).astype(jnp.float32)
    zero = jnp.zeros((sub, block_len), jnp.bfloat16)
    ids = [(side + float(g * sub)).astype(jnp.bfloat16) for g in range(TILE // 2 // sub)]
    lane = lax.broadcasted_iota(jnp.int32, (block_len, TILE), 1).astype(jnp.float32)
    keys = [lane.astype(jnp.bfloat16), (lane + float(TILE)).astype(jnp.bfloat16)]
    zeros = jnp.zeros((block_len, TILE), jnp.bfloat16)
    ones = jnp.ones((block_len, TILE), jnp.bfloat16)

    def spread(value):
        return jnp.broadcast_to(value, (sub, block_len)).astype(jnp.bfloat16)

    @pl.loop(0, block_count)
    def _(b):
        lanes = pl.ds(pl.multiple_of(b * block_len, block_len), block_len)
        turned = jnp.transpose(key_s[:, lanes])
        for d in range(det_rows):
            row_id = spread(rid_s[d : d + 1, lanes])
            qv = spread(q_s[d : d + 1, lanes])
            uv = spread(u_s[d : d + 1, lanes])
            hits = [row_id == i for i in ids]
            weighted = jnp.concatenate(
                [jnp.where(h, qv, zero) for h in hits] + [jnp.where(h, uv, zero) for h in hits],
                axis=0,
            )
            key = jnp.broadcast_to(turned[:, d : d + 1], (block_len, TILE)).astype(jnp.bfloat16)
            hot = jnp.concatenate([jnp.where(key == i, ones, zeros) for i in keys], axis=1)
            sums = jnp.dot(weighted, hot, preferred_element_type=jnp.float32)
            slot = b * det_rows + d
            sums_s[slot + 1] = sums_s[prev_s[slot]] + sums

    def tile_rows(k):
        found = sums_s[last_s[k]]
        return jnp.concatenate(
            [found[c * TILE // 2 : (c + 1) * TILE // 2, m * TILE : (m + 1) * TILE]
             for c in range(2) for m in range(2)], axis=0)

    first = jnp.concatenate([tile_rows(k) for k in range(tiles // 2)], axis=1)
    second = jnp.concatenate([tile_rows(k) for k in range(tiles // 2, tiles)], axis=1)
    for load in loads[5:]:
        load.wait()
    if direct:
        strip_at = tm * n_pol + pol
        near = det // 2 * 2 + 1 - lax.rem(det, 2)
        left = det < 2
        edge = (det == 0) | (det == n_det - 1)
        inner = (det == 1) | (det == 2)
        far = [jnp.where(left, 3 - h, h) for h in range(2)]

        def piece_rows(peer_det, r):
            peer = (peer_det * n_tm + turns[r][0]) * n_pol + turns[r][1]
            return pl.ds(pl.multiple_of(peer * kept, kept), kept)

        def send(kind, r, parity, h=0, c=0):
            peer_det = (det, near, far[h])[kind]
            if kind < 2:
                source = spec_s.at[parity, :, piece_rows(peer_det, r), :]
            else:
                peer = turns[r][0] * n_pol + turns[r][1]
                source = joined.at[parity, h, c, pl.ds(pl.multiple_of(peer * kept, kept), kept), :]
            return pltpu.make_async_remote_copy(
                src_ref=source,
                dst_ref=recv.at[kind, strip_at, parity] if kind < 2 else recv.at[2, strip_at, parity, c],
                send_sem=send_sem.at[kind + h, r, parity, c],
                recv_sem=recv_sem.at[kind, r, parity, c],
                device_id={"det": peer_det, "tm": turns[r][0], "pol": turns[r][1]},
                device_id_type=MESH,
            )

        def send_chunk(parity, h, c):
            rows = pl.ds(pl.multiple_of(far[h] * strips * kept, strips * kept), strips * kept)
            return pltpu.make_async_remote_copy(
                src_ref=spec_s.at[parity, c, rows, :],
                dst_ref=passed.at[parity, h, c],
                send_sem=chunk_send.at[parity, h, c],
                recv_sem=chunk_recv.at[parity, h, c],
                device_id={"det": near},
                device_id_type=MESH,
            )

        def send_near(parity):
            for r in range(strips):
                send(1, r, parity).start()
            for r in range(1, strips):
                send(0, r, parity).start()

    folds = [split(first + second), split(first - second)]
    starts = [jnp.where(left, KY // 2, 0), jnp.where(left, 0, KY // 2)] if direct else [0]
    count = KY // len(starts)
    for at, start in enumerate(starts):
        rows = pl.ds(pl.multiple_of(start, count), count)
        for parity, (f_high, f_low) in enumerate(folds):
            table = t_high[parity, rows, :]
            acc = lax.dot_general(table, f_high, NT, preferred_element_type=jnp.float32)
            acc = acc + lax.dot_general(table, f_low, NT, preferred_element_type=jnp.float32)
            acc = acc + lax.dot_general(
                t_low[parity, rows, :], f_high, NT, preferred_element_type=jnp.float32
            )
            for c in range(2):
                piece = acc[:, c * TILE : (c + 1) * TILE].astype(jnp.bfloat16)
                if direct:
                    spec_s[parity, c, rows, :] = piece
                else:
                    out_ref[2 * parity + c] = piece
            if direct and at:
                send_near(parity)
            elif direct:
                @pl.when(edge)
                def _():
                    for h in range(2):
                        for c in range(2):
                            send_chunk(parity, h, c).start()
    if not direct:
        return

    @pl.when(inner)
    def _():
        for parity in range(2):
            for h, c in ((0, 0), (0, 1), (1, 0), (1, 1)):
                send_chunk(parity, h, c).wait_recv()
                rows = pl.ds(pl.multiple_of(far[h] * strips * kept, strips * kept), strips * kept)
                both = passed[parity, h, c].astype(jnp.float32) + spec_s[
                    parity, c, rows, :
                ].astype(jnp.float32)
                joined[parity, h, c] = both.astype(jnp.bfloat16)
                for r in range(strips):
                    send(2, r, parity, h, c).start()

    own = pl.ds(pl.multiple_of(me * kept, kept), kept)
    for parity in range(2):
        recv[0, strip_at, parity] = spec_s[parity, :, own, :]
    for parity in range(2):
        for kind in range(3):
            for r in range(0 if kind else 1, strips):
                for c in range(2 if kind == 2 else 1):
                    send(kind, r, parity, 0, c).wait_recv()
        for strip in range(strips):
            total = recv[0, strip, parity].astype(jnp.float32)
            for kind in range(1, 3):
                total = total + recv[kind, strip, parity].astype(jnp.float32)
            for c in range(2):
                for part in range(2):
                    ordered[strip, c, part, pl.ds(parity, half, stride=2), :] = total[
                        c, part * half : (part + 1) * half
                    ]
    columns = [ordered[strip].reshape(4 * kept, TILE) for strip in range(strips)]
    x_high, x_low = split(jnp.concatenate(columns, axis=1))
    acc = jnp.dot(x_high, w_high[...], preferred_element_type=jnp.float32)
    acc = acc + jnp.dot(x_low, w_high[...], preferred_element_type=jnp.float32)
    acc = acc + jnp.dot(x_high, w_low[...], preferred_element_type=jnp.float32)
    real, imag = [], []
    for c in range(2):
        re_rows = slice(2 * c * kept, (2 * c + 1) * kept)
        im_rows = slice((2 * c + 1) * kept, (2 * c + 2) * kept)
        real.append(acc[re_rows, :length] + acc[im_rows, length:])
        imag.append(acc[im_rows, :length] - acc[re_rows, length:])
    for c in range(2):
        modes_ref[c, 0] = real[c]
        modes_ref[c, 1] = imag[c]
    for parity in range(2):
        for kind in range(2):
            for r in range(0 if kind else 1, strips):
                send(kind, r, parity).wait_send()

    @pl.when(edge)
    def _():
        for parity in range(2):
            for h in range(2):
                for c in range(2):
                    send_chunk(parity, h, c).wait_send()

    @pl.when(inner)
    def _():
        for parity in range(2):
            for h in range(2):
                for r in range(strips):
                    for c in range(2):
                        send(2, r, parity, h, c).wait_send()


def run_whole(sizes, direct, timestream, hwp_index, flags, pixel_index, tile_index, wafer, taps, angle):
    det_rows, time_len = timestream.shape
    owners = math.prod(sizes)
    strips = sizes[1] * sizes[2]
    kept = KY // owners
    length = strips * TILE
    blocks = tile_index.size
    tables = [jnp.asarray(t) for t in row_tables(owners)]
    if direct:
        tables += [jnp.asarray(t) for t in column_tables(length)]
    hwp_grid = hwp_index.reshape(time_len // LANES, LANES)
    loaded = [timestream, hwp_grid, flags, pixel_index, taps] + tables[:2]
    smem = pl.BlockSpec(memory_space=pltpu.SMEM)
    vmem = pl.BlockSpec(memory_space=pltpu.VMEM)
    hbm = pl.BlockSpec(memory_space=pl.ANY)
    wide = pltpu.VMEM((det_rows, time_len), jnp.float32)
    grid = pltpu.VMEM((time_len // LANES, LANES), jnp.float32)
    scratch = [pltpu.VMEM(x.shape, x.dtype) for x in loaded]
    scratch += [
        pltpu.SemaphoreType.DMA((9,)),
        pltpu.VMEM((det_rows, time_len + 2 * LANES), jnp.float32),
        grid, grid, wide, wide, wide, wide,
        pltpu.SMEM((blocks,), jnp.int32),
        pltpu.SMEM((MAPY // TILE,), jnp.int32),
        pltpu.VMEM((blocks + 1, TILE, 2 * TILE), jnp.float32),
        pltpu.SemaphoreType.DMA((2,)),
        pltpu.SemaphoreType.DMA((2,)),
    ]
    if direct:
        scratch += [pltpu.VMEM(x.shape, x.dtype) for x in tables[2:]]
        scratch += [
            pltpu.VMEM((2, 2, KY, TILE), jnp.bfloat16),
            pltpu.VMEM((3, strips, 2, 2, kept, TILE), jnp.bfloat16),
            pltpu.VMEM((2, 2, 2, strips * kept, TILE), jnp.bfloat16),
            pltpu.VMEM((2, 2, 2, strips * kept, TILE), jnp.bfloat16),
            pltpu.VMEM((strips, 2, 2, kept, TILE), jnp.float32),
            pltpu.SemaphoreType.DMA((4, strips, 2, 2)),
            pltpu.SemaphoreType.DMA((3, strips, 2, 2)),
            pltpu.SemaphoreType.DMA((2, 2, 2)),
            pltpu.SemaphoreType.DMA((2, 2, 2)),
        ]
        out_shape, out_specs = jax.ShapeDtypeStruct((2, 2, kept, length), jnp.float32), vmem
    else:
        out_shape, out_specs = jax.ShapeDtypeStruct((4, KY, TILE), jnp.bfloat16), vmem

    def kernel(*refs):
        whole_kernel(sizes, direct, *refs)

    return pl.pallas_call(
        kernel,
        out_shape=out_shape,
        in_specs=[smem] * 3 + [hbm] * (5 + len(tables)),
        out_specs=out_specs,
        scratch_shapes=scratch,
        compiler_params=pltpu.CompilerParams(
            collective_id=0, has_side_effects=True, vmem_limit_bytes=56 * 2**20
        ),
        name="map_to_modes",
    )(tile_index, wafer, angle, timestream, hwp_grid, flags, pixel_index, taps, *tables)


def twiddle_table(first, second, length):
    return (first * second % length).astype(jnp.float32) * (2.0 * math.pi / length)


def transform_columns(real_in, imag_in):
    lead, kept, length = real_in.shape
    outer = TILE
    inner = length // outer
    real_grid = real_in.reshape(lead, kept, outer, inner)
    imag_grid = imag_in.reshape(lead, kept, outer, inner)
    outer_pos = jnp.arange(outer, dtype=jnp.int32)
    inner_pos = jnp.arange(inner, dtype=jnp.int32)
    first_angle = twiddle_table(outer_pos[:, None], outer_pos[None, :], outer)
    first_cos = jnp.cos(first_angle)
    first_sin = jnp.sin(first_angle)
    section_real = jnp.einsum("ckab,ad->ckdb", real_grid, first_cos, precision=HIGH) + jnp.einsum(
        "ckab,ad->ckdb", imag_grid, first_sin, precision=HIGH
    )
    section_imag = jnp.einsum("ckab,ad->ckdb", imag_grid, first_cos, precision=HIGH) - jnp.einsum(
        "ckab,ad->ckdb", real_grid, first_sin, precision=HIGH
    )
    mid_angle = twiddle_table(outer_pos[:, None], inner_pos[None, :], length)
    mid_cos = jnp.cos(mid_angle)
    mid_sin = jnp.sin(mid_angle)
    turned_real = section_real * mid_cos + section_imag * mid_sin
    turned_imag = section_imag * mid_cos - section_real * mid_sin
    last_angle = twiddle_table(inner_pos[:, None], inner_pos[None, :], inner)
    last_cos = jnp.cos(last_angle)
    last_sin = jnp.sin(last_angle)
    final_real = jnp.einsum("ckdb,be->cked", turned_real, last_cos, precision=HIGH) + jnp.einsum(
        "ckdb,be->cked", turned_imag, last_sin, precision=HIGH
    )
    final_imag = jnp.einsum("ckdb,be->cked", turned_imag, last_cos, precision=HIGH) - jnp.einsum(
        "ckdb,be->cked", turned_real, last_sin, precision=HIGH
    )
    return (final_real.reshape(lead, kept, length), final_imag.reshape(lead, kept, length))


def exchange_many(spec, sizes):
    n_det, n_tm, n_pol = sizes
    owners = math.prod(sizes)
    kept = KY // owners
    half = kept // 2
    strips = n_tm * n_pol
    length = strips * TILE
    pieces = spec.reshape(2, 2, owners, 2, half, TILE)
    moved = lax.all_to_all(pieces, ("det", "tm", "pol"), split_axis=2, concat_axis=2, tiled=True)
    summed = jnp.sum(moved.reshape(2, 2, n_det, strips, 2, half, TILE).astype(jnp.float32), axis=2)
    columns = jnp.transpose(summed, (3, 1, 4, 0, 2, 5)).reshape(2, 2, kept, length)
    final_real, final_imag = transform_columns(columns[0], columns[1])
    norm_scale = 1.0 / math.sqrt(length * MAPY)
    real = final_real * norm_scale
    imag = final_imag * norm_scale
    position = (lax.axis_index("det") * n_tm + lax.axis_index("tm")) * n_pol + lax.axis_index("pol")
    cosine, sine = rotation(
        jnp.arange(length, dtype=jnp.int32)[None, :],
        length,
        (position * kept + jnp.arange(kept, dtype=jnp.int32))[:, None],
    )
    return (
        jnp.stack([cosine * real[0] + sine * real[1], cosine * imag[0] + sine * imag[1]]),
        jnp.stack([cosine * real[1] - sine * real[0], cosine * imag[1] - sine * imag[0]]),
    )


def solution(mesh):
    sizes = (mesh.shape["det"], mesh.shape["tm"], mesh.shape["pol"])
    direct = sizes[0] == 4 and KY // math.prod(sizes) % 32 == 0

    def body(*args):
        found = run_whole(sizes, direct, *args)
        if not direct:
            return exchange_many(found, sizes)
        _, _, kept, length = found.shape
        at = (lax.axis_index("det") * sizes[1] + lax.axis_index("tm")) * sizes[2]
        at = (at + lax.axis_index("pol")) * kept
        shape = (2, kept, length)
        kx = lax.broadcasted_iota(jnp.int32, shape, 2)
        cosine, sine = rotation(kx, length, at + lax.broadcasted_iota(jnp.int32, shape, 1))
        return cosine * found[0] + sine * found[1], cosine * found[1] - sine * found[0]

    in_specs = (
        P(("group", "det", "pol"), "tm"),
        P(("group", "tm")),
        P(("group", "det", "pol"), "tm"),
        P(("group", "det", "pol"), "tm"),
        P(("group", "det", "pol"), "tm"),
        P(("group", "det", "pol")),
        P(),
        P(("group", "det", "pol")),
    )
    out_specs = (
        P(None, ("group", "det", "tm", "pol"), None),
        P(None, ("group", "det", "tm", "pol"), None),
    )
    return jax.shard_map(body, mesh=mesh, in_specs=in_specs, out_specs=out_specs, check_vma=False)
```
